256 devices in a mesh: dom: 64 (over x, z, core), mp: 4 (over y).
Axes of the slice: x: 4, y: 4, z: 8, core: 2. Of those that a mesh axis runs over, the one named last changes fastest.
Arguments:
- features: bfloat16 [32768, 1024], P('dom'), may hold values from -16 to 16
- history: float32 [32768, 1024], P('dom'), may hold values from -6 to 6
- weights: bfloat16 [1024, 5, 1024], P(None, None, 'mp'), may hold values from -0.1875 to 0.1875
- cotangent: bfloat16 [32768, 1024], P('dom', 'mp'), may hold values from -6 to 6
- send_rows: int32 [64, 64, 8], P('dom'), may hold values from 0 to 1023
- neighbors: int32 [4, 32768, 8], P(None, 'dom'), may hold values from 0 to 1023
Outputs:
- output: bfloat16 [32768, 1024], P('dom', 'mp')
- grad_features: bfloat16 [32768, 1024], P('dom', 'mp')
- grad_weights: float32 [1024, 5, 1024], P('dom', None, 'mp')
The draws below stay inside these ranges and needn't reach their ends.
All inputs are finite; a program needn't handle non-finite values.
Results may differ from the reference program's by a relative error of at most 0.0052.
Values may be sent and summed in bfloat16 or wider, within the bound.
A program may use at most 128 MiB of HBM per device.

```python
import jax
import jax.numpy as jnp
from jax import lax

D = 1024
HID = 1024
RELS = 4
K = 8
ROWS = 512
HROWS = 512
SEND = 8
NODES = 32768
HIST = 32768
TABLE = 1024
N_DOM = 64


def with_ends(entries, key, smallest, high):
    longest = entries.shape.index(max(entries.shape))
    spots = []
    for shift in (0, 1):
        where = [jax.random.randint(jax.random.fold_in(key, axis), (), 0, length) for axis, length in enumerate(entries.shape)]
        where[longest] = (where[longest] + shift) % entries.shape[longest]
        spots.append(tuple(where))
    return entries.at[spots[0]].set(smallest).at[spots[1]].set(high)


def raised(result, stream_key, source, target, blocks, factor):
    def block_of(dim):
        return (jnp.arange(result.shape[dim]) // (result.shape[dim] // blocks)).reshape((-1,) + (1,) * (result.ndim - 1 - dim))

    one_side = jax.random.permutation(stream_key, blocks)[block_of(target)]
    other_side = (block_of(target) + blocks // 2) % blocks
    return jnp.where((block_of(source) == one_side) | (block_of(source) == other_side), factor * result, result)


def steps_of(own_key, shape, pieces, low, top_value):
    gain = 1.0
    for axis_at, parts in pieces:
        heights = jax.random.uniform(jax.random.fold_in(jax.random.fold_in(own_key, 6), axis_at), (parts,), jnp.float32, low / len(pieces), top_value / len(pieces))
        gain = gain * jnp.repeat(jnp.exp(heights), shape[axis_at] // parts).reshape((-1,) + (1,) * (len(shape) - 1 - axis_at))
    return gain


def bell_draw(own_key, extent, scale, bound, cuts=(), kind=jnp.bfloat16):
    drawn = jax.random.normal(own_key, extent, jnp.float32) * scale
    if len(cuts) > 0:
        drawn = steps_of(own_key, extent, cuts, -0.22, 0.18) * drawn
    return jnp.clip(drawn, min=-bound, max=bound).astype(kind)


def bell_draw_with(rng, dims, width, reach, pieces, heavy, kind=jnp.bfloat16):
    values = width * jax.random.normal(rng, dims, jnp.float32)
    if pieces:
        values = values * steps_of(rng, dims, pieces, -0.22, 0.18)
    return jnp.clip(raised(values, jax.random.fold_in(rng, 3), *heavy), -reach, reach).astype(kind)


def setup_inputs(seed: int = 0) -> dict:
    key_list = jax.random.split(jax.random.key(seed), 7)
    features = bell_draw_with(key_list[0], (NODES, D), 1.0, 16.0, ((0, 64),), (0, 1, 64, 4.0))
    history = bell_draw(key_list[1], (HIST, D), 1.0, 6.0, ((0, 64),), jnp.float32)
    weights = bell_draw(key_list[2], (D, RELS + 1, HID), D ** -0.5, 0.1875, ((2, 4),))
    cotangent = bell_draw(key_list[3], (NODES, HID), 1.0, 6.0, ((0, 64), (1, 4)))
    send_rows = with_ends(jax.random.randint(key_list[4], (N_DOM, N_DOM, SEND), 0, ROWS + HROWS), jax.random.fold_in(key_list[4], 1), 0, (ROWS + HROWS) - 1).astype(jnp.int32)
    neighbors = with_ends(jax.random.randint(key_list[5], (RELS, NODES, K), 0, TABLE), jax.random.fold_in(key_list[5], 1), 0, TABLE - 1).astype(jnp.int32)
    return {"features": features, "history": history, "weights": weights, "cotangent": cotangent, "send_rows": send_rows, "neighbors": neighbors}


def silu_slope(value):
    sigma = jax.nn.sigmoid(value)
    return sigma * (1.0 + value * (1.0 - sigma))


def reference(features, history, weights, cotangent, send_rows, neighbors):
    local_rows = features.reshape(N_DOM, ROWS, D)
    sources = jnp.concatenate([local_rows, history.reshape(N_DOM, HROWS, D).astype(jnp.bfloat16)], axis=1)
    peers = jnp.arange(N_DOM, dtype=jnp.int32)
    nbr_all = neighbors.reshape(RELS, N_DOM, ROWS, K)
    cot_all = cotangent.reshape(N_DOM, ROWS, HID)
    wide_weights = weights.astype(jnp.float32)

    def per_device(carry, index):
        halo = sources[peers[:, None], send_rows[:, index, :]]
        table = jnp.concatenate([local_rows[index], halo.reshape(N_DOM * SEND, D)], axis=0)
        nbr = nbr_all[:, index]
        aggs = []
        for r in range(RELS):
            total = jnp.zeros((ROWS, D), jnp.float32)
            for k in range(K):
                total = total + table[nbr[r][:, k]].astype(jnp.float32)
            aggs.append((total / K).astype(jnp.bfloat16))
        stack = jnp.stack(aggs + [local_rows[index]])
        pre = jnp.einsum("rnd,dro->no", stack.astype(jnp.float32), wide_weights)
        output = jax.nn.silu(pre).astype(jnp.bfloat16)
        dpre = (cot_all[index].astype(jnp.float32) * silu_slope(pre)).astype(jnp.bfloat16)
        back = jnp.einsum("no,dro->rnd", dpre.astype(jnp.float32), wide_weights)
        grad_table = jnp.zeros((TABLE, D), jnp.float32)
        grad_table = grad_table.at[:ROWS].add(back[RELS])
        for r in range(RELS):
            spread = jnp.broadcast_to(back[r][:, None, :] / K, (ROWS, K, D)).reshape(ROWS * K, D)
            grad_table = grad_table.at[nbr[r].reshape(ROWS * K)].add(spread)
        term = jnp.einsum("rnd,no->dro", stack.astype(jnp.float32), dpre.astype(jnp.float32))
        halo_grad = grad_table[ROWS:].reshape(N_DOM, SEND, D).astype(jnp.bfloat16)
        return carry + term, (output, grad_table[:ROWS], halo_grad)

    start = jnp.zeros((D, RELS + 1, HID), jnp.float32)
    grad_weights, (outputs, local_grads, halo_grads) = lax.scan(per_device, start, peers)

    def per_owner(index):
        returned = halo_grads[:, index].reshape(N_DOM * SEND, D).astype(jnp.float32)
        slots = send_rows[index].reshape(N_DOM * SEND)
        added = jnp.zeros((ROWS, D), jnp.float32).at[slots].add(returned, mode="drop")
        return (local_grads[index] + added).astype(jnp.bfloat16)

    grad_features = lax.map(per_owner, peers)
    return outputs.reshape(NODES, HID), grad_features.reshape(NODES, D), grad_weights
```

```python
import functools

import jax
import jax.numpy as jnp
from jax import lax
from jax.experimental import pallas as pl
from jax.experimental.pallas import tpu as pltpu
from jax.sharding import PartitionSpec as P

MESH = pl.DeviceIdType.MESH
CORES = 2
F32 = jnp.float32
BF16 = jnp.bfloat16


def dot(a, b):
    return jnp.dot(a, b, preferred_element_type=F32)


def dot_nt(a, b):
    return lax.dot_general(a, b, (((1,), (1,)), ((), ())), preferred_element_type=F32)


def loop(count, body):
    lax.fori_loop(0, count, lambda i, c: (body(i), c)[1], 0)


def kernel(
    X, Z, Y,
    feat, hist, w, cot, sendcol, sendrow, nbr,
    out, gf, gw,
    histv, src, asib, aown, arecv, slabs, halo, wd, nbrcol, cnt, tab, tacc, pre, tabT,
    dp, dT, eT, gsend, gown, grecv, gx, rx, gz, gzs, rz, bT, gtT, hg, ret, rets,
    hist_sem, sib_sem, halo_sem, w_sem, wf_sem, ag1_sem, ag2_sem, gc_sem, gx_sem, gz_sem, ret_sem, rsib_sem,
):
    N, D = feat.shape
    R = nbr.shape[0]
    K = nbr.shape[1]
    O = w.shape[2]
    S = D // Y
    CH = X * Z
    HR = halo.shape[1]
    SL = HR // CH
    T = N + HR
    GR = gw.shape[1]

    dom = lax.axis_index("dom")
    y = lax.axis_index("mp")
    c = lax.rem(dom, CORES)
    q = dom // CORES
    z = lax.rem(q, Z)
    x = q // Z

    def at(chip, core, yy):
        return {"dom": chip * CORES + core, "mp": yy}

    def ring(v, size):
        return lax.rem(v + size, size)

    def remote(s, d, ss, rs, dev):
        return pltpu.make_async_remote_copy(
            src_ref=s, dst_ref=d, send_sem=ss, recv_sem=rs, device_id=dev, device_id_type=MESH
        )

    sibling = at(q, 1 - c, y)
    up, down, far = ring(y + 1, Y), ring(y - 1, Y), ring(y + 2, Y)

    hist_copy = pltpu.make_async_copy(hist.at[:, pl.ds(pl.multiple_of(y * S, 128), S)], histv, hist_sem)
    hist_copy.start()

    barrier = pltpu.get_barrier_semaphore()

    def greet(dev):
        pl.semaphore_signal(barrier, inc=1, device_id=dev, device_id_type=MESH)

    greet(sibling)
    for k in range(1, Y):
        greet(at(q, c, ring(y + k, Y)))
    loop(CH - 1, lambda i: greet(at(lax.rem(q + 1 + i, CH), c, y)))

    src[0:N, :] = feat[:, pl.ds(pl.multiple_of(y * S, 128), S)]
    hist_copy.wait()
    src[N : 2 * N, :] = histv[...].astype(BF16)

    def pick(k, dst):
        step = min(128, HR)

        def body(i):
            rows = pl.ds(pl.multiple_of(i * step, step), step)
            col = sendcol[k, rows, :]
            sel = jnp.where(col == lax.broadcasted_iota(jnp.int32, (step, 2 * N), 1), 1.0, 0.0).astype(BF16)
            dst[rows, :] = dot(sel, src[...]).astype(BF16)

        loop(HR // step, body)

    pick(1, asib)
    pl.semaphore_wait(barrier, CH + Y - 1)
    sib_copy = remote(asib, arecv, sib_sem.at[0], sib_sem.at[1], sibling)
    sib_copy.start()
    pick(0, aown)
    sib_copy.wait_recv()
    slabs[...] = aown[...] + arecv[...]
    mine = pl.ds(pl.multiple_of(q * SL, SL), SL)
    halo[y, mine, :] = slabs[mine, :]

    def chip_rows(i):
        chip = lax.rem(q + 1 + i, CH)
        return chip, pl.ds(pl.multiple_of(chip * SL, SL), SL)

    def send_slab(i):
        chip, rows = chip_rows(i)
        remote(slabs.at[rows, :], halo.at[y, mine, :], halo_sem.at[0], halo_sem.at[1], at(chip, c, y)).start()

    loop(CH - 1, send_slab)
    others = pl.ds(0, HR - SL)
    halo_all = remote(slabs.at[others, :], halo.at[y, others, :], halo_sem.at[0], halo_sem.at[1], sibling)

    half = S // CORES
    w_copies = []
    for k in range(1, Y):
        to = ring(y + k, Y)
        cp = remote(
            w.at[:, pl.ds(pl.multiple_of(to * S + c * half, half), half), :],
            wd.at[y, :, pl.ds(pl.multiple_of(c * half, half), half), :],
            w_sem.at[0, k], w_sem.at[1, k], at(q, c, to),
        )
        cp.start()
        w_copies.append(cp)

    def counts(r):
        nbrcol[r] = jnp.transpose(nbr[r], (1, 0))
        step = min(32, N)

        def body(i):
            rows = pl.ds(pl.multiple_of(i * step, step), step)
            cols = nbrcol[r, rows, :]
            pos = lax.broadcasted_iota(jnp.int32, (step, T), 1)
            total = jnp.zeros((step, T), F32)
            for k in range(K):
                total = total + jnp.where(cols[:, k : k + 1] == pos, 1.0 / K, 0.0)
            cnt[r, rows, :] = total.astype(BF16)

        loop(N // step, body)

    loop(R, counts)

    def local_tab(r):
        tab[r, 0:N, :] = dot(feat[...], w[r]).astype(BF16)

    loop(R, local_tab)

    def gather_start(buf, sem):
        m = buf.shape[1] // 2
        lo, hi = pl.ds(0, m), pl.ds(m, m)
        dev_up, dev_down = at(q, c, up), at(q, c, down)

        def cp(slot, rows, k, dev):
            return remote(buf.at[slot, rows, :], buf.at[slot, rows, :], sem.at[0, k], sem.at[1, k], dev)

        copies = [
            cp(y, lo, 0, dev_up), cp(y, hi, 1, dev_down), cp(y, hi, 2, dev_up), cp(y, lo, 3, dev_down),
            cp(down, lo, 4, dev_up), cp(up, hi, 5, dev_down),
        ]
        for one in copies[:4]:
            one.start()
        return copies

    def gather_forward(copies):
        copies[0].wait_recv()
        copies[4].start()
        copies[1].wait_recv()
        copies[5].start()

    halo_all.wait_recv()
    ag1 = gather_start(halo, ag1_sem)

    pre[...] = dot(feat[...], w[R])

    def local_pre(r):
        pre[...] += dot(cnt[r, :, 0:N], tab[r, 0:N, :])

    loop(R, local_pre)
    gather_forward(ag1)

    def add_tab(slot, first):
        rows = pl.ds(pl.multiple_of(slot * S, S), S)

        def body(r):
            part = dot(halo[slot], w[r, rows, :])
            if first:
                tacc[r] = part
            else:
                tacc[r] += part

        loop(R, body)

    def turn_halo(slot):
        tabT[pl.ds(pl.multiple_of(slot * S, S), S), N:T] = jnp.transpose(halo[slot], (1, 0))

    add_tab(y, True)
    tabT[:, 0:N] = jnp.transpose(feat[...], (1, 0))
    turn_halo(y)
    ag1[2].wait_recv()
    add_tab(down, False)
    turn_halo(down)
    ag1[3].wait_recv()
    add_tab(up, False)
    turn_halo(up)
    ag1[4].wait_recv()
    ag1[5].wait_recv()
    far_rows = pl.ds(pl.multiple_of(far * S, S), S)

    def halo_pre(r):
        tab[r, N:T, :] = (tacc[r] + dot(halo[far], w[r, far_rows, :])).astype(BF16)
        pre[...] += dot(cnt[r, :, N:T], tab[r, N:T, :])

    loop(R, halo_pre)

    v = pre[...]
    s = 1.0 / (1.0 + jnp.exp(-v))
    out[...] = (v * s).astype(BF16)
    slope = (cot[...].astype(F32) * (s * (1.0 + v * (1.0 - s)))).astype(BF16)
    dp[y] = slope
    ag2 = gather_start(dp, ag2_sem)
    dT[...] = jnp.transpose(slope, (1, 0))
    turn_halo(far)

    w_forwards = []
    for k in range(1, Y):
        frm = ring(y - k, Y)
        w_copies[k - 1].wait_recv()
        part = wd.at[frm, :, pl.ds(pl.multiple_of(c * half, half), half), :]
        cp = remote(part, part, wf_sem.at[0, k], wf_sem.at[1, k], sibling)
        cp.start()
        w_forwards.append(cp)
    wd[y] = w[:, pl.ds(pl.multiple_of(y * S, S), S), :]

    def spread_units(r):
        eT[r] = dot(dT[...], cnt[r]).astype(BF16)

    loop(R, spread_units)
    gather_forward(ag2)
    tile = min(8, CH)
    span = tile * CORES * GR

    def core_copy(r):
        return remote(gsend.at[r], grecv.at[r], gc_sem.at[0, r], gc_sem.at[1, r], sibling)

    def put_terms(r, i, part):
        part = part.reshape(tile, CORES, GR, O)
        chips = pl.ds(pl.multiple_of(i * tile, tile), tile)
        gown[r, chips] = jnp.where(c == 0, part[:, 0], part[:, 1])
        gsend[r, chips] = jnp.where(c == 0, part[:, 1], part[:, 0]).astype(BF16)

    def terms(r):
        def body(i):
            rows = pl.ds(pl.multiple_of(i * span, span), span)
            put_terms(r, i, dot_nt(tabT[rows, :], eT[r]))

        loop(CH // tile, body)
        core_copy(r).start()

    loop(R, terms)

    def own_terms(i):
        rows = pl.ds(pl.multiple_of(i * span, span), span)
        put_terms(R, i, dot(tabT[rows, 0:N], dp[y]))

    loop(CH // tile, own_terms)
    core_copy(R).start()

    def x_copy(r, k):
        to = ring(x + k, X)
        return remote(
            gx.at[r, pl.ds(to * Z, Z)], rx.at[r, k - 1], gx_sem.at[0, r, k], gx_sem.at[1, r, k], at(to * Z + z, c, y)
        )

    def along_x(r):
        core_copy(r).wait_recv()

        def body(i):
            chips = pl.ds(i * tile, tile)
            total = gown[r, chips] + grecv[r, chips].astype(F32)
            gown[r, chips] = total
            gx[r, chips] = total.astype(BF16)

        loop(CH // tile, body)
        for k in range(1, X):
            x_copy(r, k).start()

    loop(R + 1, along_x)

    for k in (2, 3, 4, 5):
        ag2[k].wait_recv()
    for one in w_forwards:
        one.wait_recv()

    def back(r):
        total = dot_nt(wd[0, r], dp[0])
        for k in range(1, Y):
            total = total + dot_nt(wd[k, r], dp[k])
        return total

    def put_back(r):
        bT[r] = back(r).astype(BF16)

    loop(R, put_back)
    gtT[:, 0:N] = back(R)
    gtT[:, N:T] = dot(bT[0], cnt[0, :, N:T])
    gtT[:, 0:N] += dot(bT[0], cnt[0, :, 0:N])

    def add_table(r):
        gtT[...] += dot(bT[r + 1], cnt[r + 1])

    loop(R - 1, add_table)

    hg[...] = jnp.transpose(gtT[:, N:T], (1, 0)).astype(BF16)
    ret[mine, :] = hg[mine, :]

    def return_slab(i):
        chip, rows = chip_rows(i)
        remote(hg.at[rows, :], ret.at[mine, :], ret_sem.at[0], ret_sem.at[1], at(chip, c, y)).start()

    loop(CH - 1, return_slab)
    ret_all = remote(hg.at[others, :], ret.at[others, :], ret_sem.at[0], ret_sem.at[1], sibling)

    def z_copy(k):
        to = ring(z + k, Z)
        return remote(gzs.at[:, to], rz.at[k - 1], gz_sem.at[0, k], gz_sem.at[1, k], at(x * Z + to, c, y))

    def along_z(r):
        total = gown[r, pl.ds(x * Z, Z)]
        for k in range(1, X):
            x_copy(r, k).wait_recv()
            total = total + rx[r, k - 1].astype(F32)
        gz[r] = total
        gzs[r] = total.astype(BF16)

    loop(R + 1, along_z)
    for k in range(1, Z):
        z_copy(k).start()

    ret_all.wait_recv()
    ret_sib = remote(ret, rets, rsib_sem.at[0], rsib_sem.at[1], sibling)
    ret_sib.start()

    def owner_map(k):
        rows = lax.broadcasted_iota(jnp.int32, (N, HR), 0)
        return jnp.where(sendrow[k] == rows, 1.0, 0.0).astype(BF16)

    added = jnp.transpose(gtT[:, 0:N], (1, 0)) + dot(owner_map(0), ret[...])
    ret_sib.wait_recv()
    gf[...] = (added + dot(owner_map(1), rets[...])).astype(BF16)

    for k in range(1, Z):
        z_copy(k).wait_recv()

    def total_terms(r):
        total = gz[r, z]
        for k in range(1, Z):
            total = total + rz[k - 1, r].astype(F32)
        gw[r] = total

    loop(R + 1, total_terms)

    sib_copy.wait_send()
    halo_all.wait_send()
    ret_all.wait_send()
    ret_sib.wait_send()
    for one in w_copies + w_forwards + ag1 + ag2:
        one.wait_send()

    def sent(r):
        core_copy(r).wait_send()
        for k in range(1, X):
            x_copy(r, k).wait_send()

    loop(R + 1, sent)
    for k in range(1, Z):
        z_copy(k).wait_send()


def shards(X, Z, features, history, weights, cotangent, send_rows, neighbors):
    N, D = features.shape
    R, _, K = neighbors.shape
    O = weights.shape[2]
    Y = lax.axis_size("mp")
    S = D // Y
    CH = X * Z
    SL = CORES * send_rows.shape[2]
    HR = CH * SL
    T = N + HR
    GR = D // (CH * CORES)

    c = lax.rem(lax.axis_index("dom"), CORES)
    chosen = send_rows[0].reshape(CH, CORES, SL // CORES)
    by_core = jnp.stack([jnp.where(c == 0, chosen[:, 0], chosen[:, 1]), jnp.where(c == 0, chosen[:, 1], chosen[:, 0])])
    which = lax.broadcasted_iota(jnp.int32, (2, CH, CORES, SL // CORES), 2)
    slots = jnp.where(which == c, by_core[:, :, None, :], -1).reshape(2, HR)

    dma = pltpu.SemaphoreType.DMA
    vmem = pl.BlockSpec(memory_space=pltpu.VMEM)
    out, gf, gw = pl.pallas_call(
        functools.partial(kernel, X, Z, Y),
        out_shape=(
            jax.ShapeDtypeStruct((N, O), BF16),
            jax.ShapeDtypeStruct((N, S), BF16),
            jax.ShapeDtypeStruct((R + 1, GR, O), F32),
        ),
        in_specs=[vmem, pl.BlockSpec(memory_space=pl.ANY)] + [vmem] * 5,
        out_specs=(vmem, vmem, vmem),
        scratch_shapes=[
            pltpu.VMEM((N, S), F32),
            pltpu.VMEM((2 * N, S), BF16),
            pltpu.VMEM((HR, S), BF16),
            pltpu.VMEM((HR, S), BF16),
            pltpu.VMEM((HR, S), BF16),
            pltpu.VMEM((HR, S), BF16),
            pltpu.VMEM((Y, HR, S), BF16),
            pltpu.VMEM((Y, R + 1, S, O), BF16),
            pltpu.VMEM((R, N, K), jnp.int32),
            pltpu.VMEM((R, N, T), BF16),
            pltpu.VMEM((R, T, O), BF16),
            pltpu.VMEM((R, HR, O), F32),
            pltpu.VMEM((N, O), F32),
            pltpu.VMEM((D, T), BF16),
            pltpu.VMEM((Y, N, O), BF16),
            pltpu.VMEM((O, N), BF16),
            pltpu.VMEM((R, O, T), BF16),
            pltpu.VMEM((R + 1, CH, GR, O), BF16),
            pltpu.VMEM((R + 1, CH, GR, O), F32),
            pltpu.VMEM((R + 1, CH, GR, O), BF16),
            pltpu.VMEM((R + 1, CH, GR, O), BF16),
            pltpu.VMEM((R + 1, X - 1, Z, GR, O), BF16),
            pltpu.VMEM((R + 1, Z, GR, O), F32),
            pltpu.VMEM((R + 1, Z, GR, O), BF16),
            pltpu.VMEM((Z - 1, R + 1, GR, O), BF16),
            pltpu.VMEM((R, S, N), BF16),
            pltpu.VMEM((S, T), F32),
            pltpu.VMEM((HR, S), BF16),
            pltpu.VMEM((HR, S), BF16),
            pltpu.VMEM((HR, S), BF16),
            dma(()),
            dma((2,)),
            dma((2,)),
            dma((2, Y)),
            dma((2, Y)),
            dma((2, 6)),
            dma((2, 6)),
            dma((2, R + 1)),
            dma((2, R + 1, X)),
            dma((2, Z)),
            dma((2,)),
            dma((2,)),
        ],
        compiler_params=pltpu.CompilerParams(
            collective_id=0, has_side_effects=True, vmem_limit_bytes=58 * 1024 * 1024
        ),
        name="graph_layer",
    )(
        features,
        history,
        jnp.transpose(weights, (1, 0, 2)),
        cotangent,
        slots[:, :, None],
        slots[:, None, :],
        jnp.transpose(neighbors, (0, 2, 1)),
    )
    return out, gf, jnp.transpose(gw, (1, 0, 2))


def solution(mesh):
    in_specs = (
        P("dom", None),
        P("dom", None),
        P(None, None, "mp"),
        P("dom", "mp"),
        P("dom", None, None),
        P(None, "dom", None),
    )
    out_specs = (P("dom", "mp"), P("dom", "mp"), P("dom", None, "mp"))
    chips = mesh.shape["dom"] // CORES
    X = 4 if chips >= 8 else 2
    return jax.shard_map(
        functools.partial(shards, X, chips // X), mesh=mesh, in_specs=in_specs, out_specs=out_specs, check_vma=False
    )
```

```python
import functools

import jax
import jax.numpy as jnp
from jax import lax
from jax.experimental import pallas as pl
from jax.experimental.pallas import tpu as pltpu
from jax.sharding import PartitionSpec as P

MESH = pl.DeviceIdType.MESH
CORES = 2
F32 = jnp.float32
BF16 = jnp.bfloat16


def dot(a, b):
    return jnp.dot(a, b, preferred_element_type=F32)


def dot_nt(a, b):
    return lax.dot_general(a, b, (((1,), (1,)), ((), ())), preferred_element_type=F32)


def loop(count, body):
    lax.fori_loop(0, count, lambda i, c: (body(i), c)[1], 0)


def kernel(
    X, Z, Y,
    feat_in, hist_in, w_in, cot_in, send_in, nbr_in,
    out, gf, gw,
    feat, w, cot, nbr, sendT, tcol, sendcol, histv, src, asib, aown, arecv, slabs, halo, wd, nbrcol, cnt, tab, tacc, pre, tabT,
    dp, dT, eT, gsend, gown, grecv, gx, rx, gz, gzs, rz, bT, gtT, hg, ret, rets,
    in_sem, sib_sem, halo_sem, w_sem, wf_sem, ag1_sem, ag2_sem, gc_sem, gx_sem, gz_sem, ret_sem, rsib_sem,
):
    N, D = feat.shape
    R = nbr.shape[0]
    K = nbr.shape[1]
    O = w.shape[2]
    S = D // Y
    CH = X * Z
    HR = halo.shape[1]
    SL = HR // CH
    T = N + HR
    GR = gw.shape[1]
    SEND = SL // CORES

    dom = lax.axis_index("dom")
    y = lax.axis_index("mp")
    c = lax.rem(dom, CORES)
    q = dom // CORES
    z = lax.rem(q, Z)
    x = q // Z

    def at(chip, core, yy):
        return {"dom": chip * CORES + core, "mp": yy}

    def ring(v, size):
        return lax.rem(v + size, size)

    def remote(s, d, ss, rs, dev):
        return pltpu.make_async_remote_copy(
            src_ref=s, dst_ref=d, send_sem=ss, recv_sem=rs, device_id=dev, device_id_type=MESH
        )

    sibling = at(q, 1 - c, y)
    up, down, far = ring(y + 1, Y), ring(y - 1, Y), ring(y + 2, Y)

    pending = {}

    def wait(name):
        pending.pop(name)()

    def started(name, copy):
        copy.start()
        pending[name] = copy.wait_recv
        pending[name + " out"] = copy.wait_send
        return copy

    def finish():
        for one in list(pending):
            wait(one)

    columns = pl.ds(pl.multiple_of(y * S, 128), S)
    inputs = [
        ("send", send_in, sendT),
        ("feat slice", feat_in.at[:, columns], src.at[pl.ds(0, N), :]),
        ("hist", hist_in.at[:, columns], histv),
        ("nbr", nbr_in, nbr),
        ("feat", feat_in, feat),
        ("w", w_in, w),
        ("cot", cot_in, cot),
    ]
    for i, (name, here, there) in enumerate(inputs):
        cp = pltpu.make_async_copy(here, there, in_sem.at[i])
        cp.start()
        pending[name] = cp.wait

    barrier = pltpu.get_barrier_semaphore()

    def greet(dev):
        pl.semaphore_signal(barrier, inc=1, device_id=dev, device_id_type=MESH)

    greet(sibling)
    for k in range(1, Y):
        greet(at(q, c, ring(y + k, Y)))
    loop(CH - 1, lambda i: greet(at(lax.rem(q + 1 + i, CH), c, y)))

    wait("send")
    tcol[...] = jnp.transpose(sendT[...].astype(F32), (1, 0))
    even, odd = tcol[pl.ds(0, CH, stride=2), :], tcol[pl.ds(1, CH, stride=2), :]
    slot = lax.broadcasted_iota(jnp.int32, (CH, SL, SEND), 1)
    lane = lax.broadcasted_iota(jnp.int32, (CH, SL, SEND), 2)
    taken = slot == lane + c * SEND
    for k, rows in enumerate((jnp.where(c == 0, even, odd), jnp.where(c == 0, odd, even))):
        wide = jnp.broadcast_to(rows[:, None, :], (CH, SL, SEND))
        found = jnp.sum(jnp.where(taken, wide + 1.0, 0.0), axis=2, keepdims=True) - 1.0
        sendcol[k] = found.reshape(HR, 1).astype(jnp.int32)
    wait("feat slice")
    wait("hist")
    src[N : 2 * N, :] = histv[...].astype(BF16)

    def pick(k, dst):
        step = min(128, HR)

        def body(i):
            rows = pl.ds(pl.multiple_of(i * step, step), step)
            col = sendcol[k, rows, :]
            sel = jnp.where(col == lax.broadcasted_iota(jnp.int32, (step, 2 * N), 1), 1.0, 0.0).astype(BF16)
            dst[rows, :] = dot(sel, src[...]).astype(BF16)

        loop(HR // step, body)

    pick(1, asib)
    pl.semaphore_wait(barrier, CH + Y - 1)
    started("sib", remote(asib, arecv, sib_sem.at[0], sib_sem.at[1], sibling))
    pick(0, aown)
    wait("sib")
    slabs[...] = aown[...] + arecv[...]
    mine = pl.ds(pl.multiple_of(q * SL, SL), SL)
    halo[y, mine, :] = slabs[mine, :]

    def chip_rows(i):
        chip = lax.rem(q + 1 + i, CH)
        return chip, pl.ds(pl.multiple_of(chip * SL, SL), SL)

    def send_slab(i):
        chip, rows = chip_rows(i)
        remote(slabs.at[rows, :], halo.at[y, mine, :], halo_sem.at[0], halo_sem.at[1], at(chip, c, y)).start()

    loop(CH - 1, send_slab)
    others = pl.ds(0, HR - SL)
    halo_all = remote(slabs.at[others, :], halo.at[y, others, :], halo_sem.at[0], halo_sem.at[1], sibling)
    pending["halo"] = halo_all.wait_recv
    pending["halo out"] = halo_all.wait_send

    half = S // CORES
    wait("w")
    for k in range(1, Y):
        to = ring(y + k, Y)
        cp = remote(
            w.at[:, pl.ds(pl.multiple_of(to * S + c * half, half), half), :],
            wd.at[y, :, pl.ds(pl.multiple_of(c * half, half), half), :],
            w_sem.at[0, k], w_sem.at[1, k], at(q, c, to),
        )
        started(f"w{k}", cp)

    wait("nbr")
    def counts(r):
        nbrcol[r] = jnp.transpose(nbr[r], (1, 0))
        step = min(32, N)

        def body(i):
            rows = pl.ds(pl.multiple_of(i * step, step), step)
            cols = nbrcol[r, rows, :]
            pos = lax.broadcasted_iota(jnp.int32, (step, T), 1)
            total = jnp.zeros((step, T), F32)
            for k in range(K):
                total = total + jnp.where(cols[:, k : k + 1] == pos, 1.0 / K, 0.0)
            cnt[r, rows, :] = total.astype(BF16)

        loop(N // step, body)

    loop(R, counts)

    def local_tab(r):
        tab[r, 0:N, :] = dot(feat[...], w[r]).astype(BF16)

    wait("feat")
    loop(R, local_tab)

    def gather_start(name, buf, sem):
        m = buf.shape[1] // 2
        lo, hi = pl.ds(0, m), pl.ds(m, m)
        dev_up, dev_down = at(q, c, up), at(q, c, down)

        def cp(slot, rows, k, dev):
            return remote(buf.at[slot, rows, :], buf.at[slot, rows, :], sem.at[0, k], sem.at[1, k], dev)

        copies = [
            cp(y, lo, 0, dev_up), cp(y, hi, 1, dev_down), cp(y, hi, 2, dev_up), cp(y, lo, 3, dev_down),
            cp(down, lo, 4, dev_up), cp(up, hi, 5, dev_down),
        ]
        for k in range(4):
            started(f"{name}{k}", copies[k])
        return copies

    def gather_forward(name, copies):
        wait(f"{name}0")
        started(f"{name}4", copies[4])
        wait(f"{name}1")
        started(f"{name}5", copies[5])

    wait("halo")
    ag1 = gather_start("halo", halo, ag1_sem)

    pre[...] = dot(feat[...], w[R])

    def local_pre(r):
        pre[...] += dot(cnt[r, :, 0:N], tab[r, 0:N, :])

    loop(R, local_pre)
    gather_forward("halo", ag1)

    def add_tab(slot, first):
        rows = pl.ds(pl.multiple_of(slot * S, S), S)

        def body(r):
            part = dot(halo[slot], w[r, rows, :])
            if first:
                tacc[r] = part
            else:
                tacc[r] += part

        loop(R, body)

    def turn_halo(slot):
        tabT[pl.ds(pl.multiple_of(slot * S, S), S), N:T] = jnp.transpose(halo[slot], (1, 0))

    add_tab(y, True)
    tabT[:, 0:N] = jnp.transpose(feat[...], (1, 0))
    turn_halo(y)
    wait("halo2")
    add_tab(down, False)
    turn_halo(down)
    wait("halo3")
    add_tab(up, False)
    turn_halo(up)
    wait("halo4")
    wait("halo5")
    far_rows = pl.ds(pl.multiple_of(far * S, S), S)

    def halo_pre(r):
        tab[r, N:T, :] = (tacc[r] + dot(halo[far], w[r, far_rows, :])).astype(BF16)
        pre[...] += dot(cnt[r, :, N:T], tab[r, N:T, :])

    loop(R, halo_pre)

    v = pre[...]
    s = 1.0 / (1.0 + jnp.exp(-v))
    wait("cot")
    out[...] = (v * s).astype(BF16)
    slope = (cot[...].astype(F32) * (s * (1.0 + v * (1.0 - s)))).astype(BF16)
    dp[y] = slope
    ag2 = gather_start("dp", dp, ag2_sem)
    dT[...] = jnp.transpose(slope, (1, 0))
    turn_halo(far)

    for k in range(1, Y):
        frm = ring(y - k, Y)
        wait(f"w{k}")
        part = wd.at[frm, :, pl.ds(pl.multiple_of(c * half, half), half), :]
        started(f"wf{k}", remote(part, part, wf_sem.at[0, k], wf_sem.at[1, k], sibling))
    wd[y] = w[:, pl.ds(pl.multiple_of(y * S, S), S), :]

    def spread_units(r):
        eT[r] = dot(dT[...], cnt[r]).astype(BF16)

    loop(R, spread_units)
    gather_forward("dp", ag2)
    tile = min(8, CH)
    span = tile * CORES * GR

    def core_copy(r):
        return remote(gsend.at[r], grecv.at[r], gc_sem.at[0, r], gc_sem.at[1, r], sibling)

    def put_terms(r, i, part):
        part = part.reshape(tile, CORES, GR, O)
        chips = pl.ds(pl.multiple_of(i * tile, tile), tile)
        gown[r, chips] = jnp.where(c == 0, part[:, 0], part[:, 1])
        gsend[r, chips] = jnp.where(c == 0, part[:, 1], part[:, 0]).astype(BF16)

    def terms(r):
        def body(i):
            rows = pl.ds(pl.multiple_of(i * span, span), span)
            put_terms(r, i, dot_nt(tabT[rows, :], eT[r]))

        loop(CH // tile, body)
        core_copy(r).start()

    loop(R, terms)

    def own_terms(i):
        rows = pl.ds(pl.multiple_of(i * span, span), span)
        put_terms(R, i, dot(tabT[rows, 0:N], dp[y]))

    loop(CH // tile, own_terms)
    core_copy(R).start()
    pending["core"] = lambda: loop(R + 1, lambda r: core_copy(r).wait_recv())
    pending["core out"] = lambda: loop(R + 1, lambda r: core_copy(r).wait_send())

    def x_copy(r, k):
        to = ring(x + k, X)
        return remote(
            gx.at[r, pl.ds(to * Z, Z)], rx.at[r, k - 1], gx_sem.at[0, r, k], gx_sem.at[1, r, k], at(to * Z + z, c, y)
        )

    def along_x(r):
        core_copy(r).wait_recv()

        def body(i):
            chips = pl.ds(i * tile, tile)
            total = gown[r, chips] + grecv[r, chips].astype(F32)
            gown[r, chips] = total
            gx[r, chips] = total.astype(BF16)

        loop(CH // tile, body)
        for k in range(1, X):
            x_copy(r, k).start()

    loop(R + 1, along_x)
    pending.pop("core")

    def x_wait(r):
        for k in range(1, X):
            x_copy(r, k).wait_recv()

    def x_sent(r):
        for k in range(1, X):
            x_copy(r, k).wait_send()

    pending["x"] = lambda: loop(R + 1, x_wait)
    pending["x out"] = lambda: loop(R + 1, x_sent)

    for k in (2, 3, 4, 5):
        wait(f"dp{k}")
    for k in range(1, Y):
        wait(f"wf{k}")

    def back(r):
        total = dot_nt(wd[0, r], dp[0])
        for k in range(1, Y):
            total = total + dot_nt(wd[k, r], dp[k])
        return total

    def put_back(r):
        bT[r] = back(r).astype(BF16)

    loop(R, put_back)
    gtT[:, 0:N] = back(R)
    gtT[:, N:T] = dot(bT[0], cnt[0, :, N:T])
    gtT[:, 0:N] += dot(bT[0], cnt[0, :, 0:N])

    def add_table(r):
        gtT[...] += dot(bT[r + 1], cnt[r + 1])

    loop(R - 1, add_table)

    hg[...] = jnp.transpose(gtT[:, N:T], (1, 0)).astype(BF16)
    ret[mine, :] = hg[mine, :]

    def return_slab(i):
        chip, rows = chip_rows(i)
        remote(hg.at[rows, :], ret.at[mine, :], ret_sem.at[0], ret_sem.at[1], at(chip, c, y)).start()

    loop(CH - 1, return_slab)
    ret_all = remote(hg.at[others, :], ret.at[others, :], ret_sem.at[0], ret_sem.at[1], sibling)
    pending["ret"] = ret_all.wait_recv
    pending["ret out"] = ret_all.wait_send

    def z_copy(k):
        to = ring(z + k, Z)
        return remote(gzs.at[:, to], rz.at[k - 1], gz_sem.at[0, k], gz_sem.at[1, k], at(x * Z + to, c, y))

    def along_z(r):
        total = gown[r, pl.ds(x * Z, Z)]
        for k in range(1, X):
            x_copy(r, k).wait_recv()
            total = total + rx[r, k - 1].astype(F32)
        gz[r] = total
        gzs[r] = total.astype(BF16)

    loop(R + 1, along_z)
    pending.pop("x")
    for k in range(1, Z):
        started(f"z{k}", z_copy(k))

    wait("ret")
    started("rets", remote(ret, rets, rsib_sem.at[0], rsib_sem.at[1], sibling))

    def owner_map(k):
        rows = lax.broadcasted_iota(jnp.int32, (N, HR), 0)
        named = jnp.transpose(jnp.broadcast_to(sendcol[k], (HR, 8)), (1, 0))[0:1]
        return jnp.where(named == rows, 1.0, 0.0).astype(BF16)

    added = jnp.transpose(gtT[:, 0:N], (1, 0)) + dot(owner_map(0), ret[...])
    wait("rets")
    gf[...] = (added + dot(owner_map(1), rets[...])).astype(BF16)

    for k in range(1, Z):
        wait(f"z{k}")

    def total_terms(r):
        total = gz[r, z]
        for k in range(1, Z):
            total = total + rz[k - 1, r].astype(F32)
        gw[r] = total

    loop(R + 1, total_terms)

    finish()


def hand_out(*refs):
    sem = refs[-1]
    copies = [pltpu.make_async_copy(refs[i], refs[i + 3], sem.at[i]) for i in range(3)]
    for one in copies:
        one.start()
    for one in copies:
        one.wait()


def shards(X, Z, features, history, weights, cotangent, send_rows, neighbors):
    N, D = features.shape
    R, _, K = neighbors.shape
    O = weights.shape[2]
    Y = lax.axis_size("mp")
    S = D // Y
    CH = X * Z
    SL = CORES * send_rows.shape[2]
    HR = CH * SL
    T = N + HR
    GR = D // (CH * CORES)

    dma = pltpu.SemaphoreType.DMA
    vmem = pl.BlockSpec(memory_space=pltpu.VMEM)
    anywhere = pl.BlockSpec(memory_space=pl.ANY)
    results = pl.pallas_call(
        functools.partial(kernel, X, Z, Y),
        out_shape=(
            jax.ShapeDtypeStruct((N, O), BF16),
            jax.ShapeDtypeStruct((N, S), BF16),
            jax.ShapeDtypeStruct((R + 1, GR, O), F32),
        ),
        in_specs=[anywhere] * 6,
        out_specs=(vmem, vmem, vmem),
        scratch_shapes=[
            pltpu.VMEM((N, D), BF16),
            pltpu.VMEM((R + 1, D, O), BF16),
            pltpu.VMEM((N, O), BF16),
            pltpu.VMEM((R, K, N), jnp.int32),
            pltpu.VMEM((SL // CORES, CH * CORES), jnp.int32),
            pltpu.VMEM((CH * CORES, SL // CORES), F32),
            pltpu.VMEM((2, HR, 1), jnp.int32),
            pltpu.VMEM((N, S), F32),
            pltpu.VMEM((2 * N, S), BF16),
            pltpu.VMEM((HR, S), BF16),
            pltpu.VMEM((HR, S), BF16),
            pltpu.VMEM((HR, S), BF16),
            pltpu.VMEM((HR, S), BF16),
            pltpu.VMEM((Y, HR, S), BF16),
            pltpu.VMEM((Y, R + 1, S, O), BF16),
            pltpu.VMEM((R, N, K), jnp.int32),
            pltpu.VMEM((R, N, T), BF16),
            pltpu.VMEM((R, T, O), BF16),
            pltpu.VMEM((R, HR, O), F32),
            pltpu.VMEM((N, O), F32),
            pltpu.VMEM((D, T), BF16),
            pltpu.VMEM((Y, N, O), BF16),
            pltpu.VMEM((O, N), BF16),
            pltpu.VMEM((R, O, T), BF16),
            pltpu.VMEM((R + 1, CH, GR, O), BF16),
            pltpu.VMEM((R + 1, CH, GR, O), F32),
            pltpu.VMEM((R + 1, CH, GR, O), BF16),
            pltpu.VMEM((R + 1, CH, GR, O), BF16),
            pltpu.VMEM((R + 1, X - 1, Z, GR, O), BF16),
            pltpu.VMEM((R + 1, Z, GR, O), F32),
            pltpu.VMEM((R + 1, Z, GR, O), BF16),
            pltpu.VMEM((Z - 1, R + 1, GR, O), BF16),
            pltpu.VMEM((R, S, N), BF16),
            pltpu.VMEM((S, T), F32),
            pltpu.VMEM((HR, S), BF16),
            pltpu.VMEM((HR, S), BF16),
            pltpu.VMEM((HR, S), BF16),
            dma((7,)),
            dma((2,)),
            dma((2,)),
            dma((2, Y)),
            dma((2, Y)),
            dma((2, 6)),
            dma((2, 6)),
            dma((2, R + 1)),
            dma((2, R + 1, X)),
            dma((2, Z)),
            dma((2,)),
            dma((2,)),
        ],
        compiler_params=pltpu.CompilerParams(
            collective_id=0, has_side_effects=True, vmem_limit_bytes=58 * 1024 * 1024
        ),
        name="graph_layer",
    )(
        features,
        history,
        jnp.transpose(weights, (1, 0, 2)),
        cotangent,
        jnp.transpose(send_rows[0], (1, 0)),
        jnp.transpose(neighbors, (0, 2, 1)),
    )
    out, gf, gw = pl.pallas_call(
        hand_out,
        out_shape=tuple(jax.ShapeDtypeStruct(one.shape, one.dtype) for one in results),
        in_specs=[anywhere] * 3,
        out_specs=(anywhere,) * 3,
        scratch_shapes=[dma((3,))],
        compiler_params=pltpu.CompilerParams(vmem_limit_bytes=58 * 1024 * 1024),
        name="hand_out",
    )(*results)
    return out, gf, jnp.transpose(gw, (1, 0, 2))


def solution(mesh):
    in_specs = (
        P("dom", None),
        P("dom", None),
        P(None, None, "mp"),
        P("dom", "mp"),
        P("dom", None, None),
        P(None, "dom", None),
    )
    out_specs = (P("dom", "mp"), P("dom", "mp"), P("dom", None, "mp"))
    chips = mesh.shape["dom"] // CORES
    X = 4 if chips >= 8 else 2
    return jax.shard_map(
        functools.partial(shards, X, chips // X), mesh=mesh, in_specs=in_specs, out_specs=out_specs, check_vma=False
    )
```

```python
import functools

import jax
import jax.numpy as jnp
from jax import lax
from jax.experimental import pallas as pl
from jax.experimental.pallas import tpu as pltpu
from jax.sharding import PartitionSpec as P

MESH = pl.DeviceIdType.MESH
CORES = 2
HALVES = 2
F32 = jnp.float32
BF16 = jnp.bfloat16


def dot(a, b):
    return jnp.dot(a, b, preferred_element_type=F32)


def dot_nt(a, b):
    return lax.dot_general(a, b, (((1,), (1,)), ((), ())), preferred_element_type=F32)


def loop(count, body):
    lax.fori_loop(0, count, lambda i, c: (body(i), c)[1], 0)


def kernel(
    X, Z, Y,
    feat_in, hist_in, w_in, cot_in, send_in, nbr_in,
    out, gf, gw,
    feat, w, cot, nbr, sendT, tcol, sendcol, histv, src, asib, aown, arecv, slabs, halo, wd, nbrcol, cnt, tab, tacc, pre, tabT,
    dp, dT, eT, bacc, gsend, gown, grecv, gx, rx, gz, gzs, rz, bT, grad, owners, hg, ret, rets,
    in_sem, sib_sem, halo_sem, w_sem, wf_sem, ag1_sem, ag2_sem, gc_sem, gx_sem, gz_sem, ret_sem, rsib_sem,
):
    N, D = feat.shape
    R = nbr.shape[0]
    K = nbr.shape[1]
    O = w.shape[2]
    S = D // Y
    CH = X * Z
    HR = halo.shape[1]
    SL = HR // CH
    T = N + HR
    GR = gw.shape[1]
    SEND = SL // CORES

    dom = lax.axis_index("dom")
    y = lax.axis_index("mp")
    c = lax.rem(dom, CORES)
    q = dom // CORES
    z = lax.rem(q, Z)
    x = q // Z

    def at(chip, core, yy):
        return {"dom": chip * CORES + core, "mp": yy}

    def ring(v, size):
        return lax.rem(v + size, size)

    def remote(s, d, ss, rs, dev):
        return pltpu.make_async_remote_copy(
            src_ref=s, dst_ref=d, send_sem=ss, recv_sem=rs, device_id=dev, device_id_type=MESH
        )

    sibling = at(q, 1 - c, y)
    up, down, far = ring(y + 1, Y), ring(y - 1, Y), ring(y + 2, Y)

    pending = {}

    def wait(name):
        pending.pop(name)()

    def started(name, copy):
        copy.start()
        pending[name] = copy.wait_recv
        pending[name + " out"] = copy.wait_send
        return copy

    def finish():
        for one in list(pending):
            wait(one)

    columns = pl.ds(pl.multiple_of(y * S, 128), S)
    inputs = [
        ("send", send_in, sendT),
        ("feat slice", feat_in.at[:, columns], src.at[pl.ds(0, N), :]),
        ("hist", hist_in.at[:, columns], histv),
        ("nbr", nbr_in, nbr),
        ("feat", feat_in, feat),
        ("w", w_in, w),
        ("cot", cot_in, cot),
    ]
    for i, (name, here, there) in enumerate(inputs):
        cp = pltpu.make_async_copy(here, there, in_sem.at[i])
        cp.start()
        pending[name] = cp.wait

    barrier = pltpu.get_barrier_semaphore()

    def greet(dev):
        pl.semaphore_signal(barrier, inc=1, device_id=dev, device_id_type=MESH)

    greet(sibling)
    for k in range(1, Y):
        greet(at(q, c, ring(y + k, Y)))
    loop(CH - 1, lambda i: greet(at(lax.rem(q + 1 + i, CH), c, y)))

    wait("send")
    tcol[...] = jnp.transpose(sendT[...].astype(F32), (1, 0))
    even, odd = tcol[pl.ds(0, CH, stride=2), :], tcol[pl.ds(1, CH, stride=2), :]
    slot = lax.broadcasted_iota(jnp.int32, (CH, SL, SEND), 1)
    lane = lax.broadcasted_iota(jnp.int32, (CH, SL, SEND), 2)
    taken = slot == lane + c * SEND
    for k, rows in enumerate((jnp.where(c == 0, even, odd), jnp.where(c == 0, odd, even))):
        wide = jnp.broadcast_to(rows[:, None, :], (CH, SL, SEND))
        found = jnp.sum(jnp.where(taken, wide + 1.0, 0.0), axis=2, keepdims=True) - 1.0
        sendcol[k] = found.reshape(HR, 1).astype(jnp.int32)
    wait("feat slice")
    wait("hist")
    src[N : 2 * N, :] = histv[...].astype(BF16)

    def pick(k, dst):
        step = min(128, HR)

        def body(i):
            rows = pl.ds(pl.multiple_of(i * step, step), step)
            col = sendcol[k, rows, :]
            sel = jnp.where(col == lax.broadcasted_iota(jnp.int32, (step, 2 * N), 1), 1.0, 0.0).astype(BF16)
            dst[rows, :] = dot(sel, src[...]).astype(BF16)

        loop(HR // step, body)

    pick(1, asib)
    pl.semaphore_wait(barrier, CH + Y - 1)

    half = S // CORES
    half_rows = pl.ds(pl.multiple_of(c * half, half), half)

    def send_weights(k):
        to = ring(y + k, Y)
        rows = pl.ds(pl.multiple_of(to * S + c * half, half), half)
        part = w.at[:, rows, :]
        started(f"w{k}", remote(part, wd.at[y, :, half_rows, :], w_sem.at[0, k], w_sem.at[1, k], at(q, c, to)))

    def forward_weights(k):
        wait(f"w{k}")
        part = wd.at[ring(y - k, Y), :, half_rows, :]
        started(f"wf{k}", remote(part, part, wf_sem.at[0, k], wf_sem.at[1, k], sibling))

    wait("w")
    send_weights(1)
    send_weights(3)
    started("sib", remote(asib, arecv, sib_sem.at[0], sib_sem.at[1], sibling))
    pick(0, aown)
    wait("sib")
    slabs[...] = aown[...] + arecv[...]
    mine = pl.ds(pl.multiple_of(q * SL, SL), SL)
    halo[y, mine, :] = slabs[mine, :]

    def chip_rows(i):
        chip = lax.rem(q + 1 + i, CH)
        return chip, pl.ds(pl.multiple_of(chip * SL, SL), SL)

    others = pl.ds(0, HR - SL)
    part_cols = [pl.ds(h * (S // HALVES), S // HALVES) for h in range(HALVES)]
    for h, cols in enumerate(part_cols):
        sems = halo_sem.at[0, h], halo_sem.at[1, h]

        def send_slab(i):
            chip, rows = chip_rows(i)
            remote(slabs.at[rows, cols], halo.at[y, mine, cols], *sems, at(chip, c, y)).start()

        loop(CH - 1, send_slab)
        everything = remote(slabs.at[others, cols], halo.at[y, others, cols], *sems, sibling)
        pending[f"slabs{h}"] = everything.wait_recv
        pending[f"slabs{h} out"] = everything.wait_send

    wait("nbr")

    def counts(r):
        nbrcol[r] = jnp.transpose(nbr[r], (1, 0))
        step = min(32, N)

        def body(i):
            rows = pl.ds(pl.multiple_of(i * step, step), step)
            cols = nbrcol[r, rows, :]
            pos = lax.broadcasted_iota(jnp.int32, (step, T), 1)
            total = jnp.zeros((step, T), F32)
            for k in range(K):
                total = total + jnp.where(cols[:, k : k + 1] == pos, 1.0 / K, 0.0)
            cnt[r, rows, :] = total.astype(BF16)

        loop(N // step, body)

    def gather_start(name, buf, cols, sem):
        m = buf.shape[1] // 2
        lo, hi = pl.ds(0, m), pl.ds(m, m)
        dev_up, dev_down = at(q, c, up), at(q, c, down)

        def cp(slot, rows, k, dev):
            part = buf.at[slot, rows, cols]
            return remote(part, part, sem.at[0, k], sem.at[1, k], dev)

        copies = [
            cp(y, lo, 0, dev_up), cp(y, hi, 1, dev_down), cp(y, hi, 2, dev_up), cp(y, lo, 3, dev_down),
            cp(down, lo, 4, dev_up), cp(up, hi, 5, dev_down),
        ]
        for k in range(4):
            started(f"{name}{k}", copies[k])
        return copies

    def gather_forward(name, copies):
        wait(f"{name}0")
        started(f"{name}4", copies[4])
        wait(f"{name}1")
        started(f"{name}5", copies[5])

    def wait_halo(k):
        for h in range(HALVES):
            wait(f"halo{h}{k}")

    def local_tab(r):
        tab[r, 0:N, :] = dot(feat[...], w[r]).astype(BF16)

    def slot_rows(slot):
        return pl.ds(pl.multiple_of(slot * S, S), S)

    def turn_halo(slot):
        tabT[slot_rows(slot), N:T] = jnp.transpose(halo[slot], (1, 0))

    gathers = {}

    def gather_halo(h):
        wait(f"slabs{h}")
        gathers[h] = gather_start(f"halo{h}", halo, part_cols[h], ag1_sem.at[h])

    loop(R // 2, counts)
    gather_halo(0)
    wait("feat")
    loop(R, local_tab)
    gather_halo(1)
    gather_forward("halo0", gathers[0])
    loop(R - R // 2, lambda r: counts(r + R // 2))
    gather_forward("halo1", gathers[1])

    local = dot(feat[...], w[R])
    for r in range(R):
        local = local + dot(cnt[r, :, 0:N], tab[r, 0:N, :])
    pre[...] = local

    def own_tab(r):
        tacc[r] = dot(halo[y], w[r, slot_rows(y), :])

    def near_tab(r):
        tacc[r] += dot(halo[down], w[r, slot_rows(down), :]) + dot(halo[up], w[r, slot_rows(up), :])

    loop(R, own_tab)
    tabT[:, 0:N] = jnp.transpose(feat[...], (1, 0))
    turn_halo(y)
    wait_halo(2)
    wait_halo(3)
    loop(R, near_tab)
    turn_halo(down)
    turn_halo(up)
    wait_halo(4)
    wait_halo(5)
    send_weights(2)

    def far_tab(r):
        tab[r, N:T, :] = (tacc[r] + dot(halo[far], w[r, slot_rows(far), :])).astype(BF16)

    loop(R, far_tab)
    total = pre[...]
    for r in range(R):
        total = total + dot(cnt[r, :, N:T], tab[r, N:T, :])
    pre[...] = total

    wait("cot")
    tile = min(64, N)

    def activate(i):
        rows = pl.ds(pl.multiple_of(i * tile, tile), tile)
        v = pre[rows, :]
        s = 1.0 / (1.0 + jnp.exp(-v))
        out[rows, :] = (v * s).astype(BF16)
        dp[y, rows, :] = (cot[rows, :].astype(F32) * (s * (1.0 + v * (1.0 - s)))).astype(BF16)

    loop(N // tile, activate)
    ag2 = gather_start("dp", dp, pl.ds(0, O), ag2_sem)
    dT[...] = jnp.transpose(dp[y], (1, 0))
    turn_halo(far)

    def core_copy(p):
        return remote(gsend.at[p], grecv.at[p], gc_sem.at[0, p], gc_sem.at[1, p], sibling)

    def put_terms(p, part):
        part = part.reshape(CH, CORES, GR, O)
        gown[p] = jnp.where(c == 0, part[:, 0], part[:, 1])
        gsend[p] = jnp.where(c == 0, part[:, 1], part[:, 0]).astype(BF16)
        started(f"core{p}", core_copy(p))

    def relation_terms(r):
        eT[r] = dot(dT[...], cnt[r]).astype(BF16)
        put_terms(r + 1, dot_nt(tabT[...], eT[r]))

    def x_copy(p, k):
        to = ring(x + k, X)
        return remote(
            gx.at[p, pl.ds(to * Z, Z)], rx.at[p, k - 1], gx_sem.at[0, p, k], gx_sem.at[1, p, k], at(to * Z + z, c, y)
        )

    def along_x(p):
        wait(f"core{p}")
        some = min(8, CH)

        def body(i):
            chips = pl.ds(i * some, some)
            total = gown[p, chips] + grecv[p, chips].astype(F32)
            gown[p, chips] = total
            gx[p, chips] = total.astype(BF16)

        loop(CH // some, body)
        for k in range(1, X):
            started(f"x{p}{k}", x_copy(p, k))

    put_terms(0, dot(tabT[:, 0:N], dp[y]))
    relation_terms(0)
    along_x(0)
    gather_forward("dp", ag2)
    for r in range(1, R):
        relation_terms(r)
        along_x(r)
    forward_weights(1)
    forward_weights(3)
    along_x(R)
    forward_weights(2)

    def own_back(r):
        bacc[r] = dot_nt(w[r, slot_rows(y), :], dp[y])

    def near_back(r):
        bacc[r] += dot_nt(wd[down, r], dp[down]) + dot_nt(wd[up, r], dp[up])

    def far_back(r):
        bT[r] = (bacc[r] + dot_nt(wd[far, r], dp[far])).astype(BF16)

    loop(R + 1, own_back)
    for k in (1, 3):
        wait(f"wf{k}")
    for k in (2, 3):
        wait(f"dp{k}")
    loop(R + 1, near_back)
    wait("wf2")
    for k in (4, 5):
        wait(f"dp{k}")
    loop(R, far_back)
    received = dot(bT[0], cnt[0, :, N:T])
    for r in range(1, R):
        received = received + dot(bT[r], cnt[r, :, N:T])

    hg[...] = jnp.transpose(received, (1, 0)).astype(BF16)
    ret[mine, :] = hg[mine, :]

    def return_slab(i):
        chip, rows = chip_rows(i)
        remote(hg.at[rows, :], ret.at[mine, :], ret_sem.at[0], ret_sem.at[1], at(chip, c, y)).start()

    loop(CH - 1, return_slab)
    ret_all = remote(hg.at[others, :], ret.at[others, :], ret_sem.at[0], ret_sem.at[1], sibling)
    pending["ret"] = ret_all.wait_recv
    pending["ret out"] = ret_all.wait_send

    own = bacc[R] + dot_nt(wd[far, R], dp[far])
    for r in range(R):
        own = own + dot(bT[r], cnt[r, :, 0:N])
    grad[...] = jnp.transpose(own, (1, 0))

    def z_copy(g, places, k):
        to = ring(z + k, Z)
        return remote(
            gzs.at[places, to], rz.at[k - 1, places], gz_sem.at[0, g, k], gz_sem.at[1, g, k], at(x * Z + to, c, y)
        )

    def along_z(g, first, last):
        for p in range(first, last):
            total = gown[p, pl.ds(x * Z, Z)]
            for k in range(1, X):
                wait(f"x{p}{k}")
                total = total + rx[p, k - 1].astype(F32)
            gz[p] = total
            gzs[p] = total.astype(BF16)
        for k in range(1, Z):
            started(f"z{g}{k}", z_copy(g, pl.ds(first, last - first), k))

    first_group = (R + 2) // 2
    along_z(0, 0, first_group)

    def owner_map(k):
        rows = lax.broadcasted_iota(jnp.int32, (N, HR), 0)
        named = jnp.transpose(jnp.broadcast_to(sendcol[k], (HR, 8)), (1, 0))[0:1]
        return jnp.where(named == rows, 1.0, 0.0).astype(BF16)

    for k in range(2):
        owners[k] = owner_map(k)
    along_z(1, first_group, R + 1)

    wait("ret")
    started("rets", remote(ret, rets, rsib_sem.at[0], rsib_sem.at[1], sibling))
    grad[...] += dot(owners[0], ret[...])
    wait("rets")
    gf[...] = (grad[...] + dot(owners[1], rets[...])).astype(BF16)

    def total_terms(p, r):
        total = gz[p, z]
        for k in range(1, Z):
            total = total + rz[k - 1, p].astype(F32)
        gw[r] = total

    for k in range(1, Z):
        wait(f"z0{k}")
        wait(f"z1{k}")
    total_terms(0, R)
    loop(R, lambda r: total_terms(r + 1, r))
    finish()


def hand_out(*refs):
    for here, there in zip(refs[:3], refs[3:]):
        there[...] = here[...]


def shards(X, Z, features, history, weights, cotangent, send_rows, neighbors):
    N, D = features.shape
    R, _, K = neighbors.shape
    O = weights.shape[2]
    Y = lax.axis_size("mp")
    S = D // Y
    CH = X * Z
    SL = CORES * send_rows.shape[2]
    HR = CH * SL
    T = N + HR
    GR = D // (CH * CORES)

    dma = pltpu.SemaphoreType.DMA
    vmem = pl.BlockSpec(memory_space=pltpu.VMEM)
    anywhere = pl.BlockSpec(memory_space=pl.ANY)
    results = pl.pallas_call(
        functools.partial(kernel, X, Z, Y),
        out_shape=(
            jax.ShapeDtypeStruct((N, O), BF16),
            jax.ShapeDtypeStruct((N, S), BF16),
            jax.ShapeDtypeStruct((R + 1, GR, O), F32),
        ),
        in_specs=[anywhere] * 6,
        out_specs=(vmem, vmem, vmem),
        scratch_shapes=[
            pltpu.VMEM((N, D), BF16),
            pltpu.VMEM((R + 1, D, O), BF16),
            pltpu.VMEM((N, O), BF16),
            pltpu.VMEM((R, K, N), jnp.int32),
            pltpu.VMEM((SL // CORES, CH * CORES), jnp.int32),
            pltpu.VMEM((CH * CORES, SL // CORES), F32),
            pltpu.VMEM((2, HR, 1), jnp.int32),
            pltpu.VMEM((N, S), F32),
            pltpu.VMEM((2 * N, S), BF16),
            pltpu.VMEM((HR, S), BF16),
            pltpu.VMEM((HR, S), BF16),
            pltpu.VMEM((HR, S), BF16),
            pltpu.VMEM((HR, S), BF16),
            pltpu.VMEM((Y, HR, S), BF16),
            pltpu.VMEM((Y, R + 1, S, O), BF16),
            pltpu.VMEM((R, N, K), jnp.int32),
            pltpu.VMEM((R, N, T), BF16),
            pltpu.VMEM((R, T, O), BF16),
            pltpu.VMEM((R, HR, O), F32),
            pltpu.VMEM((N, O), F32),
            pltpu.VMEM((D, T), BF16),
            pltpu.VMEM((Y, N, O), BF16),
            pltpu.VMEM((O, N), BF16),
            pltpu.VMEM((R, O, T), BF16),
            pltpu.VMEM((R + 1, S, N), F32),
            pltpu.VMEM((R + 1, CH, GR, O), BF16),
            pltpu.VMEM((R + 1, CH, GR, O), F32),
            pltpu.VMEM((R + 1, CH, GR, O), BF16),
            pltpu.VMEM((R + 1, CH, GR, O), BF16),
            pltpu.VMEM((R + 1, X - 1, Z, GR, O), BF16),
            pltpu.VMEM((R + 1, Z, GR, O), F32),
            pltpu.VMEM((R + 1, Z, GR, O), BF16),
            pltpu.VMEM((Z - 1, R + 1, GR, O), BF16),
            pltpu.VMEM((R, S, N), BF16),
            pltpu.VMEM((N, S), F32),
            pltpu.VMEM((2, N, HR), BF16),
            pltpu.VMEM((HR, S), BF16),
            pltpu.VMEM((HR, S), BF16),
            pltpu.VMEM((HR, S), BF16),
            dma((7,)),
            dma((2,)),
            dma((2, HALVES)),
            dma((2, Y)),
            dma((2, Y)),
            dma((HALVES, 2, 6)),
            dma((2, 6)),
            dma((2, R + 1)),
            dma((2, R + 1, X)),
            dma((2, 2, Z)),
            dma((2,)),
            dma((2,)),
        ],
        compiler_params=pltpu.CompilerParams(
            collective_id=0, has_side_effects=True, vmem_limit_bytes=58 * 1024 * 1024
        ),
        name="graph_layer",
    )(
        features,
        history,
        jnp.transpose(weights, (1, 0, 2)),
        cotangent,
        jnp.transpose(send_rows[0], (1, 0)),
        jnp.transpose(neighbors, (0, 2, 1)),
    )
    out, gf, gw = pl.pallas_call(
        hand_out,
        out_shape=tuple(jax.ShapeDtypeStruct(one.shape, one.dtype) for one in results),
        in_specs=[vmem] * 3,
        out_specs=(vmem,) * 3,
        name="hand_out",
    )(*results)
    return out, gf, jnp.transpose(gw, (1, 0, 2))


def solution(mesh):
    in_specs = (
        P("dom", None),
        P("dom", None),
        P(None, None, "mp"),
        P("dom", "mp"),
        P("dom", None, None),
        P(None, "dom", None),
    )
    out_specs = (P("dom", "mp"), P("dom", "mp"), P("dom", None, "mp"))
    chips = mesh.shape["dom"] // CORES
    X = 4 if chips >= 8 else 2
    return jax.shard_map(
        functools.partial(shards, X, chips // X), mesh=mesh, in_specs=in_specs, out_specs=out_specs, check_vma=False
    )
```

```python
import functools

import jax
import jax.numpy as jnp
from jax import lax
from jax.experimental import pallas as pl
from jax.experimental.pallas import tpu as pltpu
from jax.sharding import PartitionSpec as P

MESH = pl.DeviceIdType.MESH
CORES = 2
HALVES = 2
F32 = jnp.float32
BF16 = jnp.bfloat16


def dot(a, b):
    return jnp.dot(a, b, preferred_element_type=F32)


def dot_nt(a, b):
    return lax.dot_general(a, b, (((1,), (1,)), ((), ())), preferred_element_type=F32)


def loop(count, body):
    lax.fori_loop(0, count, lambda i, c: (body(i), c)[1], 0)


def kernel(
    X, Z, Y,
    feat_in, hist_in, w_in, cot_in, send_in, nbr_in,
    out, gf, gw,
    feat, w, cot, nbr, sendT, tcol, sendcol, histv, src, asib, aown, arecv, slabs, halo, wd, nbrcol, cnt, tab, tacc, pre, tabT,
    dp, dT, eT, bacc, gsend, gown, grecv, gx, relay, rx, gz, gzs, rz, bT, grad, owners, hg, ret, rets,
    in_sem, sib_sem, halo_sem, w_sem, wf_sem, ag1_sem, ag2_sem, gc_sem, gr_sem, gx_sem, gz_sem, ret_sem, rsib_sem,
):
    N, D = feat.shape
    R = nbr.shape[0]
    K = nbr.shape[1]
    O = w.shape[2]
    S = D // Y
    CH = X * Z
    HR = halo.shape[1]
    SL = HR // CH
    T = N + HR
    GR = gw.shape[1]
    SEND = SL // CORES

    dom = lax.axis_index("dom")
    y = lax.axis_index("mp")
    c = lax.rem(dom, CORES)
    q = dom // CORES
    z = lax.rem(q, Z)
    x = q // Z

    def at(chip, core, yy):
        return {"dom": chip * CORES + core, "mp": yy}

    def ring(v, size):
        return lax.rem(v + size, size)

    def remote(s, d, ss, rs, dev):
        return pltpu.make_async_remote_copy(
            src_ref=s, dst_ref=d, send_sem=ss, recv_sem=rs, device_id=dev, device_id_type=MESH
        )

    sibling = at(q, 1 - c, y)
    up, down, far = ring(y + 1, Y), ring(y - 1, Y), ring(y + 2, Y)

    pending = {}

    def wait(name):
        pending.pop(name)()

    def started(name, copy):
        copy.start()
        pending[name] = copy.wait_recv
        pending[name + " out"] = copy.wait_send
        return copy

    def finish():
        for one in list(pending):
            wait(one)

    columns = pl.ds(pl.multiple_of(y * S, 128), S)
    inputs = [
        ("send", send_in, sendT),
        ("feat slice", feat_in.at[:, columns], src.at[pl.ds(0, N), :]),
        ("hist", hist_in.at[:, columns], histv),
        ("nbr", nbr_in, nbr),
        ("feat", feat_in, feat),
        ("w", w_in, w),
        ("cot", cot_in, cot),
    ]
    for i, (name, here, there) in enumerate(inputs):
        cp = pltpu.make_async_copy(here, there, in_sem.at[i])
        cp.start()
        pending[name] = cp.wait

    barrier = pltpu.get_barrier_semaphore()

    def greet(dev):
        pl.semaphore_signal(barrier, inc=1, device_id=dev, device_id_type=MESH)

    greet(sibling)
    for k in range(1, Y):
        greet(at(q, c, ring(y + k, Y)))
    loop(CH - 1, lambda i: greet(at(lax.rem(q + 1 + i, CH), c, y)))

    wait("send")
    tcol[...] = jnp.transpose(sendT[...].astype(F32), (1, 0))
    even, odd = tcol[pl.ds(0, CH, stride=2), :], tcol[pl.ds(1, CH, stride=2), :]
    slot = lax.broadcasted_iota(jnp.int32, (CH, SL, SEND), 1)
    lane = lax.broadcasted_iota(jnp.int32, (CH, SL, SEND), 2)
    taken = slot == lane + c * SEND
    for k, rows in enumerate((jnp.where(c == 0, even, odd), jnp.where(c == 0, odd, even))):
        wide = jnp.broadcast_to(rows[:, None, :], (CH, SL, SEND))
        found = jnp.sum(jnp.where(taken, wide + 1.0, 0.0), axis=2, keepdims=True) - 1.0
        sendcol[k] = found.reshape(HR, 1).astype(jnp.int32)
    wait("feat slice")
    wait("hist")
    src[N : 2 * N, :] = histv[...].astype(BF16)

    def pick(k, dst):
        step = min(256, HR)

        def body(i):
            rows = pl.ds(i * step, step)
            col = sendcol[k, rows, :]
            sel = jnp.where(col == lax.broadcasted_iota(jnp.int32, (step, 2 * N), 1), 1.0, 0.0).astype(BF16)
            dst[rows, :] = dot(sel, src[...]).astype(BF16)

        for i in range(HR // step):
            body(i)

    pick(1, asib)
    pl.semaphore_wait(barrier, CH + Y - 1)

    half = S // CORES
    half_rows = pl.ds(pl.multiple_of(c * half, half), half)

    def send_weights(k):
        to = ring(y + k, Y)
        rows = pl.ds(pl.multiple_of(to * S + c * half, half), half)
        part = w.at[:, rows, :]
        started(f"w{k}", remote(part, wd.at[y, :, half_rows, :], w_sem.at[0, k], w_sem.at[1, k], at(q, c, to)))

    def forward_weights(k):
        wait(f"w{k}")
        part = wd.at[ring(y - k, Y), :, half_rows, :]
        started(f"wf{k}", remote(part, part, wf_sem.at[0, k], wf_sem.at[1, k], sibling))

    wait("w")
    send_weights(1)
    send_weights(3)
    send_weights(2)
    started("sib", remote(asib, arecv, sib_sem.at[0], sib_sem.at[1], sibling))
    pick(0, aown)
    wait("sib")
    slabs[...] = aown[...] + arecv[...]
    mine = pl.ds(pl.multiple_of(q * SL, SL), SL)
    halo[y, mine, :] = slabs[mine, :]

    def chip_rows(i):
        chip = lax.rem(q + 1 + i, CH)
        return chip, pl.ds(pl.multiple_of(chip * SL, SL), SL)

    others = pl.ds(0, HR - SL)
    part_cols = [pl.ds(h * (S // HALVES), S // HALVES) for h in range(HALVES)]
    for h, cols in enumerate(part_cols):
        sems = halo_sem.at[0, h], halo_sem.at[1, h]

        def send_slab(i):
            chip, rows = chip_rows(i)
            remote(slabs.at[rows, cols], halo.at[y, mine, cols], *sems, at(chip, c, y)).start()

        loop(CH - 1, send_slab)
        everything = remote(slabs.at[others, cols], halo.at[y, others, cols], *sems, sibling)
        pending[f"slabs{h}"] = everything.wait_recv
        pending[f"slabs{h} out"] = everything.wait_send

    wait("nbr")

    def counts(r):
        nbrcol[r] = jnp.transpose(nbr[r], (1, 0))
        step = min(128, N)
        share, none = jnp.asarray(1.0 / K, BF16), jnp.asarray(0.0, BF16)

        def body(i):
            rows = pl.ds(pl.multiple_of(i * step, step), step)
            cols = nbrcol[r, rows, :].astype(jnp.int16)
            pos = lax.broadcasted_iota(jnp.int16, (step, T), 1)
            total = jnp.zeros((step, T), BF16)
            for k in range(K):
                total = total + jnp.where(jnp.broadcast_to(cols[:, k : k + 1], (step, T)) == pos, share, none)
            cnt[r, rows, :] = total

        loop(N // step, body)

    def gather_start(name, buf, cols, sem):
        m = buf.shape[1] // 2
        lo, hi = pl.ds(0, m), pl.ds(m, m)
        dev_up, dev_down = at(q, c, up), at(q, c, down)

        def cp(slot, rows, k, dev):
            part = buf.at[slot, rows, cols]
            return remote(part, part, sem.at[0, k], sem.at[1, k], dev)

        copies = [
            cp(y, lo, 0, dev_up), cp(y, hi, 1, dev_down), cp(y, hi, 2, dev_up), cp(y, lo, 3, dev_down),
            cp(down, lo, 4, dev_up), cp(up, hi, 5, dev_down),
        ]
        for k in range(4):
            started(f"{name}{k}", copies[k])
        return copies

    def gather_forward(name, copies):
        wait(f"{name}0")
        started(f"{name}4", copies[4])
        wait(f"{name}1")
        started(f"{name}5", copies[5])

    def wait_halo(k):
        for h in range(HALVES):
            wait(f"halo{h}{k}")

    def local_tab(r):
        tab[r, 0:N, :] = dot(feat[...], w[r]).astype(BF16)

    def slot_rows(slot):
        return pl.ds(pl.multiple_of(slot * S, S), S)

    def turn_halo(slot):
        tabT[slot_rows(slot), N:T] = jnp.transpose(halo[slot], (1, 0))

    gathers = {}

    def gather_halo(h):
        wait(f"slabs{h}")
        gathers[h] = gather_start(f"halo{h}", halo, part_cols[h], ag1_sem.at[h])

    loop(R, counts)
    wait("feat")
    gather_halo(0)
    loop(R, local_tab)
    gather_halo(1)
    gather_forward("halo0", gathers[0])

    local = dot(feat[...], w[R])
    for r in range(R):
        local = local + dot(cnt[r, :, 0:N], tab[r, 0:N, :])
    pre[...] = local
    gather_forward("halo1", gathers[1])

    def own_tab(r):
        tacc[r] = dot(halo[y], w[r, slot_rows(y), :])

    def near_tab(r):
        tacc[r] += dot(halo[down], w[r, slot_rows(down), :]) + dot(halo[up], w[r, slot_rows(up), :])

    loop(R, own_tab)
    tabT[:, 0:N] = jnp.transpose(feat[...], (1, 0))
    turn_halo(y)
    wait_halo(2)
    wait_halo(3)
    loop(R, near_tab)
    turn_halo(down)
    turn_halo(up)
    wait_halo(4)
    wait_halo(5)

    def far_tab(r):
        tab[r, N:T, :] = (tacc[r] + dot(halo[far], w[r, slot_rows(far), :])).astype(BF16)

    for r in range(R):
        far_tab(r)
    total = pre[...]
    for r in range(R):
        total = total + dot(cnt[r, :, N:T], tab[r, N:T, :])
    pre[...] = total

    wait("cot")
    tile = min(128, N)

    def activate(i):
        rows = pl.ds(pl.multiple_of(i * tile, tile), tile)
        v = pre[rows, :]
        s = 1.0 / (1.0 + jnp.exp(-v))
        out[rows, :] = (v * s).astype(BF16)
        dp[y, rows, :] = (cot[rows, :].astype(F32) * (s * (1.0 + v * (1.0 - s)))).astype(BF16)

    loop(N // tile, activate)
    ag2 = gather_start("dp", dp, pl.ds(0, O), ag2_sem)
    dT[...] = jnp.transpose(dp[y], (1, 0))
    turn_halo(far)

    def core_copy(p):
        return remote(gsend.at[p], grecv.at[p], gc_sem.at[0, p], gc_sem.at[1, p], sibling)

    def put_terms(p, part):
        part = part.reshape(CH, CORES, GR, O)
        gown[p] = jnp.where(c == 0, part[:, 0], part[:, 1])
        gsend[p] = jnp.where(c == 0, part[:, 1], part[:, 0]).astype(BF16)
        started(f"core{p}", core_copy(p))

    def relation_terms(r):
        eT[r] = dot(dT[...], cnt[r]).astype(BF16)
        put_terms(r + 1, dot_nt(tabT[...], eT[r]))

    x_up, x_down, x_far = ring(x + 1, X), ring(x - 1, X), ring(x + 2, X)
    zh = Z // 2

    def x_copy(p, k, block, to):
        return remote(block, rx.at[p, k], gx_sem.at[0, p, k], gx_sem.at[1, p, k], at(to * Z + z, c, y))

    def far_x(p):
        wait(f"core{p}")
        some = min(8, CH)

        def body(i):
            chips = pl.ds(i * some, some)
            total = gown[p, chips] + grecv[p, chips].astype(F32)
            gown[p, chips] = total
            gx[p, chips] = total.astype(BF16)

        loop(CH // some, body)
        for k, to in enumerate((x_up, x_down)):
            block = gx.at[p, pl.ds(x_far * Z + k * zh, zh)]
            sems = gr_sem.at[0, p, k], gr_sem.at[1, p, k]
            started(f"r{p}{k}", remote(block, relay.at[p, k], *sems, at(to * Z + z, c, y)))

    def near_x(p):
        for k, to in enumerate((x_up, x_down)):
            wait(f"r{p}{k}")
            part = pl.ds(to * Z + k * zh, zh)
            gx[p, part] = (gown[p, part] + relay[p, k].astype(F32)).astype(BF16)
            started(f"x{p}{k}", x_copy(p, k, gx.at[p, pl.ds(to * Z, Z)], to))

    put_terms(0, dot(tabT[:, 0:N], dp[y]))
    relation_terms(0)
    far_x(0)
    relation_terms(1)
    far_x(1)
    gather_forward("dp", ag2)
    near_x(0)
    for r in range(2, R):
        relation_terms(r)
        far_x(r)
        near_x(r - 1)
    far_x(R)
    forward_weights(1)
    forward_weights(3)
    near_x(R - 1)
    forward_weights(2)

    def own_back(r):
        bacc[r] = dot_nt(w[r, slot_rows(y), :], dp[y])

    def near_back(r):
        bacc[r] += dot_nt(wd[down, r], dp[down]) + dot_nt(wd[up, r], dp[up])

    def far_back(r):
        bT[r] = (bacc[r] + dot_nt(wd[far, r], dp[far])).astype(BF16)

    loop(R + 1, own_back)
    near_x(R)
    for k in (1, 3):
        wait(f"wf{k}")
    for k in (2, 3):
        wait(f"dp{k}")
    loop(R + 1, near_back)
    wait("wf2")
    for k in (4, 5):
        wait(f"dp{k}")
    for r in range(R):
        far_back(r)
    received = dot(bT[0], cnt[0, :, N:T])
    for r in range(1, R):
        received = received + dot(bT[r], cnt[r, :, N:T])

    hg[...] = jnp.transpose(received, (1, 0)).astype(BF16)
    ret[mine, :] = hg[mine, :]

    def return_slab(i):
        chip, rows = chip_rows(i)
        remote(hg.at[rows, :], ret.at[mine, :], ret_sem.at[0], ret_sem.at[1], at(chip, c, y)).start()

    loop(CH - 1, return_slab)
    ret_all = remote(hg.at[others, :], ret.at[others, :], ret_sem.at[0], ret_sem.at[1], sibling)
    pending["ret"] = ret_all.wait_recv
    pending["ret out"] = ret_all.wait_send

    own = bacc[R] + dot_nt(wd[far, R], dp[far])
    for r in range(R):
        own = own + dot(bT[r], cnt[r, :, 0:N])
    grad[...] = jnp.transpose(own, (1, 0))

    def z_copy(g, places, k):
        to = ring(z + k, Z)
        return remote(
            gzs.at[places, to], rz.at[k - 1, places], gz_sem.at[0, g, k], gz_sem.at[1, g, k], at(x * Z + to, c, y)
        )

    def along_z(g, first, last):
        for p in range(first, last):
            total = gown[p, pl.ds(x * Z, Z)]
            for k in range(2):
                wait(f"x{p}{k}")
                total = total + rx[p, k].astype(F32)
            gz[p] = total
            gzs[p] = total.astype(BF16)
        for k in range(1, Z):
            started(f"z{g}{k}", z_copy(g, pl.ds(first, last - first), k))

    first_group = (R + 2) // 2
    along_z(0, 0, first_group)

    def owner_map(k):
        rows = lax.broadcasted_iota(jnp.int32, (N, HR), 0)
        named = jnp.transpose(jnp.broadcast_to(sendcol[k], (HR, 8)), (1, 0))[0:1]
        return jnp.where(named == rows, 1.0, 0.0).astype(BF16)

    for k in range(2):
        owners[k] = owner_map(k)
    along_z(1, first_group, R + 1)

    wait("ret")
    started("rets", remote(ret, rets, rsib_sem.at[0], rsib_sem.at[1], sibling))
    grad[...] += dot(owners[0], ret[...])
    wait("rets")
    gf[...] = (grad[...] + dot(owners[1], rets[...])).astype(BF16)

    def total_terms(p, r):
        total = gz[p, z]
        for k in range(1, Z):
            total = total + rz[k - 1, p].astype(F32)
        gw[r] = total

    for k in range(1, Z):
        wait(f"z0{k}")
        wait(f"z1{k}")
    total_terms(0, R)
    loop(R, lambda r: total_terms(r + 1, r))
    finish()


def hand_out(*refs):
    for here, there in zip(refs[:3], refs[3:]):
        there[...] = here[...]


def shards(X, Z, features, history, weights, cotangent, send_rows, neighbors):
    N, D = features.shape
    R, _, K = neighbors.shape
    O = weights.shape[2]
    Y = lax.axis_size("mp")
    S = D // Y
    CH = X * Z
    SL = CORES * send_rows.shape[2]
    HR = CH * SL
    T = N + HR
    GR = D // (CH * CORES)

    dma = pltpu.SemaphoreType.DMA
    vmem = pl.BlockSpec(memory_space=pltpu.VMEM)
    anywhere = pl.BlockSpec(memory_space=pl.ANY)
    results = pl.pallas_call(
        functools.partial(kernel, X, Z, Y),
        out_shape=(
            jax.ShapeDtypeStruct((N, O), BF16),
            jax.ShapeDtypeStruct((N, S), BF16),
            jax.ShapeDtypeStruct((R + 1, GR, O), F32),
        ),
        in_specs=[anywhere] * 6,
        out_specs=(vmem, vmem, vmem),
        scratch_shapes=[
            pltpu.VMEM((N, D), BF16),
            pltpu.VMEM((R + 1, D, O), BF16),
            pltpu.VMEM((N, O), BF16),
            pltpu.VMEM((R, K, N), jnp.int32),
            pltpu.VMEM((SL // CORES, CH * CORES), jnp.int32),
            pltpu.VMEM((CH * CORES, SL // CORES), F32),
            pltpu.VMEM((2, HR, 1), jnp.int32),
            pltpu.VMEM((N, S), F32),
            pltpu.VMEM((2 * N, S), BF16),
            pltpu.VMEM((HR, S), BF16),
            pltpu.VMEM((HR, S), BF16),
            pltpu.VMEM((HR, S), BF16),
            pltpu.VMEM((HR, S), BF16),
            pltpu.VMEM((Y, HR, S), BF16),
            pltpu.VMEM((Y, R + 1, S, O), BF16),
            pltpu.VMEM((R, N, K), jnp.int32),
            pltpu.VMEM((R, N, T), BF16),
            pltpu.VMEM((R, T, O), BF16),
            pltpu.VMEM((R, HR, O), F32),
            pltpu.VMEM((N, O), F32),
            pltpu.VMEM((D, T), BF16),
            pltpu.VMEM((Y, N, O), BF16),
            pltpu.VMEM((O, N), BF16),
            pltpu.VMEM((R, O, T), BF16),
            pltpu.VMEM((R + 1, S, N), F32),
            pltpu.VMEM((R + 1, CH, GR, O), BF16),
            pltpu.VMEM((R + 1, CH, GR, O), F32),
            pltpu.VMEM((R + 1, CH, GR, O), BF16),
            pltpu.VMEM((R + 1, CH, GR, O), BF16),
            pltpu.VMEM((R + 1, 2, Z // 2, GR, O), BF16),
            pltpu.VMEM((R + 1, 2, Z, GR, O), BF16),
            pltpu.VMEM((R + 1, Z, GR, O), F32),
            pltpu.VMEM((R + 1, Z, GR, O), BF16),
            pltpu.VMEM((Z - 1, R + 1, GR, O), BF16),
            pltpu.VMEM((R, S, N), BF16),
            pltpu.VMEM((N, S), F32),
            pltpu.VMEM((2, N, HR), BF16),
            pltpu.VMEM((HR, S), BF16),
            pltpu.VMEM((HR, S), BF16),
            pltpu.VMEM((HR, S), BF16),
            dma((7,)),
            dma((2,)),
            dma((2, HALVES)),
            dma((2, Y)),
            dma((2, Y)),
            dma((HALVES, 2, 6)),
            dma((2, 6)),
            dma((2, R + 1)),
            dma((2, R + 1, 2)),
            dma((2, R + 1, 2)),
            dma((2, 2, Z)),
            dma((2,)),
            dma((2,)),
        ],
        compiler_params=pltpu.CompilerParams(
            collective_id=0, has_side_effects=True, vmem_limit_bytes=58 * 1024 * 1024
        ),
        name="graph_layer",
    )(
        features,
        history,
        jnp.transpose(weights, (1, 0, 2)),
        cotangent,
        jnp.transpose(send_rows[0], (1, 0)),
        jnp.transpose(neighbors, (0, 2, 1)),
    )
    out, gf, gw = pl.pallas_call(
        hand_out,
        out_shape=tuple(jax.ShapeDtypeStruct(one.shape, one.dtype) for one in results),
        in_specs=[vmem] * 3,
        out_specs=(vmem,) * 3,
        name="hand_out",
    )(*results)
    return out, gf, jnp.transpose(gw, (1, 0, 2))


def solution(mesh):
    in_specs = (
        P("dom", None),
        P("dom", None),
        P(None, None, "mp"),
        P("dom", "mp"),
        P("dom", None, None),
        P(None, "dom", None),
    )
    out_specs = (P("dom", "mp"), P("dom", "mp"), P("dom", None, "mp"))
    chips = mesh.shape["dom"] // CORES
    X = 4 if chips >= 8 else 2
    return jax.shard_map(
        functools.partial(shards, X, chips // X), mesh=mesh, in_specs=in_specs, out_specs=out_specs, check_vma=False
    )
```

```python
import functools

import jax
import jax.numpy as jnp
from jax import lax
from jax.experimental import pallas as pl
from jax.experimental.pallas import tpu as pltpu
from jax.sharding import PartitionSpec as P

MESH = pl.DeviceIdType.MESH
CORES = 2
HALVES = 2
F32 = jnp.float32
BF16 = jnp.bfloat16


def dot(a, b):
    return jnp.dot(a, b, preferred_element_type=F32)


def dot_nt(a, b):
    return lax.dot_general(a, b, (((1,), (1,)), ((), ())), preferred_element_type=F32)


def loop(count, body):
    lax.fori_loop(0, count, lambda i, c: (body(i), c)[1], 0)


def kernel(
    X, Z, Y,
    feat_in, hist_in, w_in, cot_in, send_in, nbr_in,
    out, gf, gw,
    feat, w, cot, nbr, sendT, tcol, sendcol, histv, src, asib, aown, arecv, slabs, halo, wd, nbrcol, cnt, tab, tacc, pre, tabT,
    dp, dT, eT, bacc, gsend, gown, grecv, gx, relay, rx, gz, gzs, rz, bT, grad, owners, hg, ret, rets,
    in_sem, sib_sem, halo_sem, w_sem, wx_sem, wf_sem, ag1_sem, ag2_sem, gc_sem, gr_sem, gx_sem, gz_sem, ret_sem, rsib_sem,
):
    N, D = feat.shape
    R = nbr.shape[0]
    K = nbr.shape[1]
    O = w.shape[2]
    S = D // Y
    CH = X * Z
    HR = halo.shape[1]
    SL = HR // CH
    T = N + HR
    GR = gw.shape[1]
    SEND = SL // CORES

    dom = lax.axis_index("dom")
    y = lax.axis_index("mp")
    c = lax.rem(dom, CORES)
    q = dom // CORES
    z = lax.rem(q, Z)
    x = q // Z

    def at(chip, core, yy):
        return {"dom": chip * CORES + core, "mp": yy}

    def ring(v, size):
        return lax.rem(v + size, size)

    def remote(s, d, ss, rs, dev):
        return pltpu.make_async_remote_copy(
            src_ref=s, dst_ref=d, send_sem=ss, recv_sem=rs, device_id=dev, device_id_type=MESH
        )

    sibling = at(q, 1 - c, y)
    up, down, far = ring(y + 1, Y), ring(y - 1, Y), ring(y + 2, Y)

    pending = {}

    def wait(name):
        pending.pop(name)()

    def started(name, copy):
        copy.start()
        pending[name] = copy.wait_recv
        pending[name + " out"] = copy.wait_send
        return copy

    def finish():
        for one in list(pending):
            wait(one)

    columns = pl.ds(pl.multiple_of(y * S, 128), S)
    inputs = [
        ("send", send_in, sendT),
        ("feat slice", feat_in.at[:, columns], src.at[pl.ds(0, N), :]),
        ("hist", hist_in.at[:, columns], histv),
        ("nbr", nbr_in, nbr),
        ("feat", feat_in, feat),
        ("w", w_in, w),
        ("cot", cot_in, cot),
    ]
    for i, (name, here, there) in enumerate(inputs):
        cp = pltpu.make_async_copy(here, there, in_sem.at[i])
        cp.start()
        pending[name] = cp.wait

    barrier = pltpu.get_barrier_semaphore()

    def greet(dev):
        pl.semaphore_signal(barrier, inc=1, device_id=dev, device_id_type=MESH)

    greet(sibling)
    for k in range(1, Y):
        greet(at(q, c, ring(y + k, Y)))
    loop(CH - 1, lambda i: greet(at(lax.rem(q + 1 + i, CH), c, y)))

    wait("send")
    tcol[...] = jnp.transpose(sendT[...].astype(F32), (1, 0))
    even, odd = tcol[pl.ds(0, CH, stride=2), :], tcol[pl.ds(1, CH, stride=2), :]
    slot = lax.broadcasted_iota(jnp.int32, (CH, SL, SEND), 1)
    lane = lax.broadcasted_iota(jnp.int32, (CH, SL, SEND), 2)
    taken = slot == lane + c * SEND
    for k, rows in enumerate((jnp.where(c == 0, even, odd), jnp.where(c == 0, odd, even))):
        wide = jnp.broadcast_to(rows[:, None, :], (CH, SL, SEND))
        found = jnp.sum(jnp.where(taken, wide + 1.0, 0.0), axis=2, keepdims=True) - 1.0
        sendcol[k] = found.reshape(HR, 1).astype(jnp.int32)
    wait("feat slice")
    wait("hist")
    src[N : 2 * N, :] = histv[...].astype(BF16)

    def pick(k, dst):
        step = min(256, HR)

        def body(i):
            rows = pl.ds(i * step, step)
            col = jnp.broadcast_to(sendcol[k, rows, :].astype(jnp.int16), (step, 2 * N))
            named = col == lax.broadcasted_iota(jnp.int16, (step, 2 * N), 1)
            sel = jnp.where(named, jnp.asarray(1.0, BF16), jnp.asarray(0.0, BF16))
            dst[rows, :] = dot(sel, src[...]).astype(BF16)

        for i in range(HR // step):
            body(i)

    pick(1, asib)
    pl.semaphore_wait(barrier, CH + Y - 1)

    half = S // CORES
    piece = half // X
    half_rows = pl.ds(pl.multiple_of(c * half, half), half)
    piece_rows = pl.ds(pl.multiple_of(c * half + x * piece, piece), piece)

    def send_weights(k):
        to = ring(y + k, Y)
        rows = pl.ds(pl.multiple_of(to * S + c * half + x * piece, piece), piece)
        sems = w_sem.at[0, k], w_sem.at[1, k]
        started(f"w{k}", remote(w.at[:, rows, :], wd.at[k - 1, :, piece_rows, :], *sems, at(q, c, to)))

    def share_weights():
        for k in range(1, Y):
            wait(f"w{k}")
        part = wd.at[:, :, piece_rows, :]
        for k in range(1, X):
            to = at(ring(x + k, X) * Z + z, c, y)
            started(f"wx{k}", remote(part, part, wx_sem.at[0, k], wx_sem.at[1, k], to))

    def pass_weights():
        for k in range(1, X):
            wait(f"wx{k}")
        part = wd.at[:, :, half_rows, :]
        started("wf", remote(part, part, wf_sem.at[0], wf_sem.at[1], sibling))

    wait("w")
    send_weights(1)
    send_weights(3)
    send_weights(2)
    started("sib", remote(asib, arecv, sib_sem.at[0], sib_sem.at[1], sibling))
    pick(0, aown)
    wait("sib")
    slabs[...] = aown[...] + arecv[...]
    mine = pl.ds(pl.multiple_of(q * SL, SL), SL)
    halo[y, mine, :] = slabs[mine, :]

    def chip_rows(i):
        chip = lax.rem(q + 1 + i, CH)
        return chip, pl.ds(pl.multiple_of(chip * SL, SL), SL)

    others = pl.ds(0, HR - SL)
    part_cols = [pl.ds(h * (S // HALVES), S // HALVES) for h in range(HALVES)]
    for h, cols in enumerate(part_cols):
        sems = halo_sem.at[0, h], halo_sem.at[1, h]

        def send_slab(i):
            chip, rows = chip_rows(i)
            remote(slabs.at[rows, cols], halo.at[y, mine, cols], *sems, at(chip, c, y)).start()

        loop(CH - 1, send_slab)
        everything = remote(slabs.at[others, cols], halo.at[y, others, cols], *sems, sibling)
        pending[f"slabs{h}"] = everything.wait_recv
        pending[f"slabs{h} out"] = everything.wait_send

    wait("nbr")

    def counts(r):
        nbrcol[r] = jnp.transpose(nbr[r], (1, 0))
        step = min(128, N)
        share, none = jnp.asarray(1.0 / K, BF16), jnp.asarray(0.0, BF16)

        def body(i):
            rows = pl.ds(pl.multiple_of(i * step, step), step)
            cols = nbrcol[r, rows, :].astype(jnp.int16)
            pos = lax.broadcasted_iota(jnp.int16, (step, T), 1)
            total = jnp.zeros((step, T), BF16)
            for k in range(K):
                total = total + jnp.where(jnp.broadcast_to(cols[:, k : k + 1], (step, T)) == pos, share, none)
            cnt[r, rows, :] = total

        loop(N // step, body)

    def gather_start(name, buf, cols, sem):
        m = buf.shape[1] // 2
        lo, hi = pl.ds(0, m), pl.ds(m, m)
        dev_up, dev_down = at(q, c, up), at(q, c, down)

        def cp(slot, rows, k, dev):
            part = buf.at[slot, rows, cols]
            return remote(part, part, sem.at[0, k], sem.at[1, k], dev)

        copies = [
            cp(y, lo, 0, dev_up), cp(y, hi, 1, dev_down), cp(y, hi, 2, dev_up), cp(y, lo, 3, dev_down),
            cp(down, lo, 4, dev_up), cp(up, hi, 5, dev_down),
        ]
        for k in range(4):
            started(f"{name}{k}", copies[k])
        return copies

    def gather_forward(name, copies):
        wait(f"{name}0")
        started(f"{name}4", copies[4])
        wait(f"{name}1")
        started(f"{name}5", copies[5])

    def wait_halo(k):
        for h in range(HALVES):
            wait(f"halo{h}{k}")

    def local_tab(r):
        tab[r, 0:N, :] = dot(feat[...], w[r]).astype(BF16)

    def slot_rows(slot):
        return pl.ds(pl.multiple_of(slot * S, S), S)

    def turn_halo(slot):
        tabT[slot_rows(slot), N:T] = jnp.transpose(halo[slot], (1, 0))

    gathers = {}

    def gather_halo(h):
        wait(f"slabs{h}")
        gathers[h] = gather_start(f"halo{h}", halo, part_cols[h], ag1_sem.at[h])

    loop(R, counts)
    wait("feat")
    gather_halo(0)
    loop(R, local_tab)
    gather_halo(1)
    gather_forward("halo0", gathers[0])
    share_weights()

    local = dot(feat[...], w[R])
    for r in range(R):
        local = local + dot(cnt[r, :, 0:N], tab[r, 0:N, :])
    pre[...] = local
    gather_forward("halo1", gathers[1])

    def own_tab(r):
        tacc[r] = dot(halo[y], w[r, slot_rows(y), :])

    def near_tab(r):
        tacc[r] += dot(halo[down], w[r, slot_rows(down), :]) + dot(halo[up], w[r, slot_rows(up), :])

    loop(R, own_tab)
    tabT[:, 0:N] = jnp.transpose(feat[...], (1, 0))
    turn_halo(y)
    wait_halo(2)
    wait_halo(3)
    loop(R, near_tab)
    turn_halo(down)
    turn_halo(up)
    wait_halo(4)
    wait_halo(5)

    def far_tab(r):
        tab[r, N:T, :] = (tacc[r] + dot(halo[far], w[r, slot_rows(far), :])).astype(BF16)

    for r in range(R):
        far_tab(r)
    total = pre[...]
    for r in range(R):
        total = total + dot(cnt[r, :, N:T], tab[r, N:T, :])
    pre[...] = total

    wait("cot")
    tile = min(128, N)

    def activate(i):
        rows = pl.ds(pl.multiple_of(i * tile, tile), tile)
        v = pre[rows, :]
        s = 1.0 / (1.0 + jnp.exp(-v))
        out[rows, :] = (v * s).astype(BF16)
        dp[y, rows, :] = (cot[rows, :].astype(F32) * (s * (1.0 + v * (1.0 - s)))).astype(BF16)

    loop(N // tile, activate)
    ag2 = [
        remote(dp.at[slot, rows, :], dp.at[slot, rows, :], ag2_sem.at[0, k], ag2_sem.at[1, k], at(q, c, to))
        for k, (slot, first, count, to) in enumerate((
            (y, 0, 1, up), (y, 2, 1, down), (y, 1, 1, up), (y, 3, 1, down), (y, 2, 2, up), (y, 0, 2, down),
            (down, 0, 1, up), (up, 2, 1, down), (down, 1, 1, up), (up, 3, 1, down),
        ))
        for rows in [pl.ds(first * (N // 4), count * (N // 4))]
    ]
    for k in range(6):
        started(f"dp{k}", ag2[k])

    def forward_dp(k):
        wait(f"dp{k}")
        started(f"dp{k + 6}", ag2[k + 6])

    dT[...] = jnp.transpose(dp[y], (1, 0))
    turn_halo(far)

    def core_copy(p):
        return remote(gsend.at[p], grecv.at[p], gc_sem.at[0, p], gc_sem.at[1, p], sibling)

    def put_terms(p, part):
        part = part.reshape(CH, CORES, GR, O)
        gown[p] = jnp.where(c == 0, part[:, 0], part[:, 1])
        gsend[p] = jnp.where(c == 0, part[:, 1], part[:, 0]).astype(BF16)
        started(f"core{p}", core_copy(p))

    def relation_terms(r):
        eT[r] = dot(dT[...], cnt[r]).astype(BF16)
        put_terms(r + 1, dot_nt(tabT[...], eT[r]))

    x_up, x_down, x_far = ring(x + 1, X), ring(x - 1, X), ring(x + 2, X)
    zh = Z // 2

    def x_copy(p, k, block, to):
        return remote(block, rx.at[p, k], gx_sem.at[0, p, k], gx_sem.at[1, p, k], at(to * Z + z, c, y))

    def far_x(p):
        wait(f"core{p}")
        some = min(8, CH)

        def body(i):
            chips = pl.ds(i * some, some)
            total = gown[p, chips] + grecv[p, chips].astype(F32)
            gown[p, chips] = total
            gx[p, chips] = total.astype(BF16)

        loop(CH // some, body)
        for k, to in enumerate((x_up, x_down)):
            block = gx.at[p, pl.ds(x_far * Z + k * zh, zh)]
            sems = gr_sem.at[0, p, k], gr_sem.at[1, p, k]
            started(f"r{p}{k}", remote(block, relay.at[p, k], *sems, at(to * Z + z, c, y)))

    def near_x(p):
        for k, to in enumerate((x_up, x_down)):
            wait(f"r{p}{k}")
            part = pl.ds(to * Z + k * zh, zh)
            gx[p, part] = (gown[p, part] + relay[p, k].astype(F32)).astype(BF16)
            started(f"x{p}{k}", x_copy(p, k, gx.at[p, pl.ds(to * Z, Z)], to))

    put_terms(0, dot(tabT[:, 0:N], dp[y]))
    relation_terms(0)
    far_x(0)
    pass_weights()
    relation_terms(1)
    far_x(1)
    forward_dp(0)
    forward_dp(1)
    near_x(0)
    for r in range(2, R):
        relation_terms(r)
        far_x(r)
        if r == 2:
            forward_dp(2)
            forward_dp(3)
        near_x(r - 1)
    far_x(R)
    near_x(R - 1)

    def own_back(r):
        bacc[r] = dot_nt(w[r, slot_rows(y), :], dp[y])

    def near_back(r):
        bacc[r] += dot_nt(wd[0, r], dp[down]) + dot_nt(wd[2, r], dp[up])

    def far_back(r):
        bT[r] = (bacc[r] + dot_nt(wd[1, r], dp[far])).astype(BF16)

    loop(R + 1, own_back)
    near_x(R)
    wait("wf")
    for k in (4, 5):
        wait(f"dp{k}")
    loop(R + 1, near_back)
    for k in (6, 7, 8, 9):
        wait(f"dp{k}")
    for r in range(R):
        far_back(r)
    received = dot(bT[0], cnt[0, :, N:T])
    for r in range(1, R):
        received = received + dot(bT[r], cnt[r, :, N:T])

    hg[...] = jnp.transpose(received, (1, 0)).astype(BF16)
    ret[mine, :] = hg[mine, :]

    def return_slab(i):
        chip, rows = chip_rows(i)
        remote(hg.at[rows, :], ret.at[mine, :], ret_sem.at[0], ret_sem.at[1], at(chip, c, y)).start()

    loop(CH - 1, return_slab)
    ret_all = remote(hg.at[others, :], ret.at[others, :], ret_sem.at[0], ret_sem.at[1], sibling)
    pending["ret"] = ret_all.wait_recv
    pending["ret out"] = ret_all.wait_send

    own = bacc[R] + dot_nt(wd[1, R], dp[far])
    for r in range(R):
        own = own + dot(bT[r], cnt[r, :, 0:N])
    grad[...] = jnp.transpose(own, (1, 0))

    def z_copy(g, places, k):
        to = ring(z + k, Z)
        return remote(
            gzs.at[places, to], rz.at[k - 1, places], gz_sem.at[0, g, k], gz_sem.at[1, g, k], at(x * Z + to, c, y)
        )

    def along_z(g, first, last):
        for p in range(first, last):
            total = gown[p, pl.ds(x * Z, Z)]
            for k in range(2):
                wait(f"x{p}{k}")
                total = total + rx[p, k].astype(F32)
            gz[p] = total
            gzs[p] = total.astype(BF16)
        for k in range(1, Z):
            started(f"z{g}{k}", z_copy(g, pl.ds(first, last - first), k))

    first_group = (R + 2) // 2
    along_z(0, 0, first_group)

    def owner_map(k):
        rows = lax.broadcasted_iota(jnp.int32, (N, HR), 0)
        named = jnp.transpose(jnp.broadcast_to(sendcol[k], (HR, 8)), (1, 0))[0:1]
        return jnp.where(named == rows, 1.0, 0.0).astype(BF16)

    for k in range(2):
        owners[k] = owner_map(k)
    along_z(1, first_group, R + 1)

    wait("ret")
    started("rets", remote(ret, rets, rsib_sem.at[0], rsib_sem.at[1], sibling))
    grad[...] += dot(owners[0], ret[...])
    wait("rets")
    gf[...] = (grad[...] + dot(owners[1], rets[...])).astype(BF16)

    def total_terms(p, r):
        total = gz[p, z]
        for k in range(1, Z):
            total = total + rz[k - 1, p].astype(F32)
        gw[r] = total

    for k in range(1, Z):
        wait(f"z0{k}")
        wait(f"z1{k}")
    total_terms(0, R)
    loop(R, lambda r: total_terms(r + 1, r))
    finish()


def hand_out(*refs):
    for here, there in zip(refs[:3], refs[3:]):
        there[...] = here[...]


def shards(X, Z, features, history, weights, cotangent, send_rows, neighbors):
    N, D = features.shape
    R, _, K = neighbors.shape
    O = weights.shape[2]
    Y = lax.axis_size("mp")
    S = D // Y
    CH = X * Z
    SL = CORES * send_rows.shape[2]
    HR = CH * SL
    T = N + HR
    GR = D // (CH * CORES)

    dma = pltpu.SemaphoreType.DMA
    vmem = pl.BlockSpec(memory_space=pltpu.VMEM)
    anywhere = pl.BlockSpec(memory_space=pl.ANY)
    results = pl.pallas_call(
        functools.partial(kernel, X, Z, Y),
        out_shape=(
            jax.ShapeDtypeStruct((N, O), BF16),
            jax.ShapeDtypeStruct((N, S), BF16),
            jax.ShapeDtypeStruct((R + 1, GR, O), F32),
        ),
        in_specs=[anywhere] * 6,
        out_specs=(vmem, vmem, vmem),
        scratch_shapes=[
            pltpu.VMEM((N, D), BF16),
            pltpu.VMEM((R + 1, D, O), BF16),
            pltpu.VMEM((N, O), BF16),
            pltpu.VMEM((R, K, N), jnp.int32),
            pltpu.VMEM((SL // CORES, CH * CORES), jnp.int32),
            pltpu.VMEM((CH * CORES, SL // CORES), F32),
            pltpu.VMEM((2, HR, 1), jnp.int32),
            pltpu.VMEM((N, S), F32),
            pltpu.VMEM((2 * N, S), BF16),
            pltpu.VMEM((HR, S), BF16),
            pltpu.VMEM((HR, S), BF16),
            pltpu.VMEM((HR, S), BF16),
            pltpu.VMEM((HR, S), BF16),
            pltpu.VMEM((Y, HR, S), BF16),
            pltpu.VMEM((Y - 1, R + 1, S, O), BF16),
            pltpu.VMEM((R, N, K), jnp.int32),
            pltpu.VMEM((R, N, T), BF16),
            pltpu.VMEM((R, T, O), BF16),
            pltpu.VMEM((R, HR, O), F32),
            pltpu.VMEM((N, O), F32),
            pltpu.VMEM((D, T), BF16),
            pltpu.VMEM((Y, N, O), BF16),
            pltpu.VMEM((O, N), BF16),
            pltpu.VMEM((R, O, T), BF16),
            pltpu.VMEM((R + 1, S, N), F32),
            pltpu.VMEM((R + 1, CH, GR, O), BF16),
            pltpu.VMEM((R + 1, CH, GR, O), F32),
            pltpu.VMEM((R + 1, CH, GR, O), BF16),
            pltpu.VMEM((R + 1, CH, GR, O), BF16),
            pltpu.VMEM((R + 1, 2, Z // 2, GR, O), BF16),
            pltpu.VMEM((R + 1, 2, Z, GR, O), BF16),
            pltpu.VMEM((R + 1, Z, GR, O), F32),
            pltpu.VMEM((R + 1, Z, GR, O), BF16),
            pltpu.VMEM((Z - 1, R + 1, GR, O), BF16),
            pltpu.VMEM((R, S, N), BF16),
            pltpu.VMEM((N, S), F32),
            pltpu.VMEM((2, N, HR), BF16),
            pltpu.VMEM((HR, S), BF16),
            pltpu.VMEM((HR, S), BF16),
            pltpu.VMEM((HR, S), BF16),
            dma((7,)),
            dma((2,)),
            dma((2, HALVES)),
            dma((2, Y)),
            dma((2, X)),
            dma((2,)),
            dma((HALVES, 2, 6)),
            dma((2, 10)),
            dma((2, R + 1)),
            dma((2, R + 1, 2)),
            dma((2, R + 1, 2)),
            dma((2, 2, Z)),
            dma((2,)),
            dma((2,)),
        ],
        compiler_params=pltpu.CompilerParams(
            collective_id=0, has_side_effects=True, vmem_limit_bytes=58 * 1024 * 1024
        ),
        name="graph_layer",
    )(
        features,
        history,
        jnp.transpose(weights, (1, 0, 2)),
        cotangent,
        jnp.transpose(send_rows[0], (1, 0)),
        jnp.transpose(neighbors, (0, 2, 1)),
    )
    out, gf, gw = pl.pallas_call(
        hand_out,
        out_shape=tuple(jax.ShapeDtypeStruct(one.shape, one.dtype) for one in results),
        in_specs=[vmem] * 3,
        out_specs=(vmem,) * 3,
        name="hand_out",
    )(*results)
    return out, gf, jnp.transpose(gw, (1, 0, 2))


def solution(mesh):
    in_specs = (
        P("dom", None),
        P("dom", None),
        P(None, None, "mp"),
        P("dom", "mp"),
        P("dom", None, None),
        P(None, "dom", None),
    )
    out_specs = (P("dom", "mp"), P("dom", "mp"), P("dom", None, "mp"))
    chips = mesh.shape["dom"] // CORES
    X = 4 if chips >= 8 else 2
    return jax.shard_map(
        functools.partial(shards, X, chips // X), mesh=mesh, in_specs=in_specs, out_specs=out_specs, check_vma=False
    )
```

```python
import functools

import jax
import jax.numpy as jnp
from jax import lax
from jax.experimental import pallas as pl
from jax.experimental.pallas import tpu as pltpu
from jax.sharding import PartitionSpec as P

MESH = pl.DeviceIdType.MESH
CORES = 2
HALVES = 2
F32 = jnp.float32
BF16 = jnp.bfloat16


def dot(a, b):
    return jnp.dot(a, b, preferred_element_type=F32)


def dot_nt(a, b):
    return lax.dot_general(a, b, (((1,), (1,)), ((), ())), preferred_element_type=F32)


def loop(count, body):
    lax.fori_loop(0, count, lambda i, c: (body(i), c)[1], 0)


def kernel(
    X, Z, Y,
    feat_in, hist_in, w_in, cot_in, send_in, nbr_in,
    out, gf, gw,
    feat, w, cot, nbr, sendT, tcol, sendcol, histv, src, asib, aown, arecv, slabs, halo, wd, nbrcol, cnt, tab, tacc, pre, tabT,
    dp, dT, eT, bacc, gsend, gown, grecv, gx, relay, rx, gz, gzs, rz, lz, lzr, lsum, lx, lxr, bT, grad, owners, hg, ret, rets,
    in_sem, sib_sem, halo_sem, w_sem, wx_sem, wf_sem, ag1_sem, ag2_sem, gc_sem, gr_sem, gx_sem, gz_sem, lz_sem, lx_sem, ret_sem, rsib_sem,
):
    N, D = feat.shape
    R = nbr.shape[0]
    K = nbr.shape[1]
    O = w.shape[2]
    S = D // Y
    CH = X * Z
    HR = halo.shape[1]
    SL = HR // CH
    T = N + HR
    GR = gw.shape[1]
    SEND = SL // CORES

    dom = lax.axis_index("dom")
    y = lax.axis_index("mp")
    c = lax.rem(dom, CORES)
    q = dom // CORES
    z = lax.rem(q, Z)
    x = q // Z

    def at(chip, core, yy):
        return {"dom": chip * CORES + core, "mp": yy}

    def ring(v, size):
        return lax.rem(v + size, size)

    def remote(s, d, ss, rs, dev):
        return pltpu.make_async_remote_copy(
            src_ref=s, dst_ref=d, send_sem=ss, recv_sem=rs, device_id=dev, device_id_type=MESH
        )

    sibling = at(q, 1 - c, y)
    up, down, far = ring(y + 1, Y), ring(y - 1, Y), ring(y + 2, Y)

    pending = {}

    def wait(name):
        pending.pop(name)()

    def started(name, copy):
        copy.start()
        pending[name] = copy.wait_recv
        pending[name + " out"] = copy.wait_send
        return copy

    def finish():
        for one in list(pending):
            wait(one)

    columns = pl.ds(pl.multiple_of(y * S, 128), S)
    inputs = [
        ("send", send_in, sendT),
        ("feat slice", feat_in.at[:, columns], src.at[pl.ds(0, N), :]),
        ("hist", hist_in.at[:, columns], histv),
        ("nbr", nbr_in, nbr),
        ("feat", feat_in, feat),
        ("w", w_in, w),
        ("cot", cot_in, cot),
    ]
    for i, (name, here, there) in enumerate(inputs):
        cp = pltpu.make_async_copy(here, there, in_sem.at[i])
        cp.start()
        pending[name] = cp.wait

    barrier = pltpu.get_barrier_semaphore()

    def greet(dev):
        pl.semaphore_signal(barrier, inc=1, device_id=dev, device_id_type=MESH)

    greet(sibling)
    for k in range(1, Y):
        greet(at(q, c, ring(y + k, Y)))
    loop(CH - 1, lambda i: greet(at(lax.rem(q + 1 + i, CH), c, y)))

    wait("send")
    tcol[...] = jnp.transpose(sendT[...].astype(F32), (1, 0))
    even, odd = tcol[pl.ds(0, CH, stride=2), :], tcol[pl.ds(1, CH, stride=2), :]
    slot = lax.broadcasted_iota(jnp.int32, (CH, SL, SEND), 1)
    lane = lax.broadcasted_iota(jnp.int32, (CH, SL, SEND), 2)
    taken = slot == lane + c * SEND
    for k, rows in enumerate((jnp.where(c == 0, even, odd), jnp.where(c == 0, odd, even))):
        wide = jnp.broadcast_to(rows[:, None, :], (CH, SL, SEND))
        found = jnp.sum(jnp.where(taken, wide + 1.0, 0.0), axis=2, keepdims=True) - 1.0
        sendcol[k] = found.reshape(HR, 1).astype(jnp.int32)
    wait("feat slice")
    wait("hist")
    src[N : 2 * N, :] = histv[...].astype(BF16)

    def pick(k, dst):
        step = min(256, HR)

        def body(i):
            rows = pl.ds(i * step, step)
            col = jnp.broadcast_to(sendcol[k, rows, :].astype(jnp.int16), (step, 2 * N))
            named = col == lax.broadcasted_iota(jnp.int16, (step, 2 * N), 1)
            sel = jnp.where(named, jnp.asarray(1.0, BF16), jnp.asarray(0.0, BF16))
            dst[rows, :] = dot(sel, src[...]).astype(BF16)

        for i in range(HR // step):
            body(i)

    pick(1, asib)
    pl.semaphore_wait(barrier, CH + Y - 1)

    half = S // CORES
    piece = half // X
    half_rows = pl.ds(pl.multiple_of(c * half, half), half)
    piece_rows = pl.ds(pl.multiple_of(c * half + x * piece, piece), piece)

    def send_weights(k):
        to = ring(y + k, Y)
        rows = pl.ds(pl.multiple_of(to * S + c * half + x * piece, piece), piece)
        sems = w_sem.at[0, k], w_sem.at[1, k]
        started(f"w{k}", remote(w.at[:, rows, :], wd.at[k - 1, :, piece_rows, :], *sems, at(q, c, to)))

    def share_weights():
        for k in range(1, Y):
            wait(f"w{k}")
        part = wd.at[:, :, piece_rows, :]
        for k in range(1, X):
            to = at(ring(x + k, X) * Z + z, c, y)
            started(f"wx{k}", remote(part, part, wx_sem.at[0, k], wx_sem.at[1, k], to))

    def pass_weights():
        for k in range(1, X):
            wait(f"wx{k}")
        part = wd.at[:, :, half_rows, :]
        started("wf", remote(part, part, wf_sem.at[0], wf_sem.at[1], sibling))

    wait("w")
    send_weights(1)
    send_weights(3)
    send_weights(2)
    started("sib", remote(asib, arecv, sib_sem.at[0], sib_sem.at[1], sibling))
    pick(0, aown)
    wait("sib")
    slabs[...] = aown[...] + arecv[...]
    mine = pl.ds(pl.multiple_of(q * SL, SL), SL)
    halo[y, mine, :] = slabs[mine, :]

    def chip_rows(i):
        chip = lax.rem(q + 1 + i, CH)
        return chip, pl.ds(pl.multiple_of(chip * SL, SL), SL)

    others = pl.ds(0, HR - SL)
    part_cols = [pl.ds(h * (S // HALVES), S // HALVES) for h in range(HALVES)]
    for h, cols in enumerate(part_cols):
        sems = halo_sem.at[0, h], halo_sem.at[1, h]

        def send_slab(i):
            chip, rows = chip_rows(i)
            remote(slabs.at[rows, cols], halo.at[y, mine, cols], *sems, at(chip, c, y)).start()

        loop(CH - 1, send_slab)
        everything = remote(slabs.at[others, cols], halo.at[y, others, cols], *sems, sibling)
        pending[f"slabs{h}"] = everything.wait_recv
        pending[f"slabs{h} out"] = everything.wait_send

    wait("nbr")

    def counts(r):
        nbrcol[r] = jnp.transpose(nbr[r], (1, 0))
        step = min(128, N)
        share, none = jnp.asarray(1.0 / K, BF16), jnp.asarray(0.0, BF16)

        def body(i):
            rows = pl.ds(pl.multiple_of(i * step, step), step)
            cols = nbrcol[r, rows, :].astype(jnp.int16)
            pos = lax.broadcasted_iota(jnp.int16, (step, T), 1)
            total = jnp.zeros((step, T), BF16)
            for k in range(K):
                total = total + jnp.where(jnp.broadcast_to(cols[:, k : k + 1], (step, T)) == pos, share, none)
            cnt[r, rows, :] = total

        loop(N // step, body)

    def gather_start(name, buf, cols, sem):
        m = buf.shape[1] // 2
        lo, hi = pl.ds(0, m), pl.ds(m, m)
        dev_up, dev_down = at(q, c, up), at(q, c, down)

        def cp(slot, rows, k, dev):
            part = buf.at[slot, rows, cols]
            return remote(part, part, sem.at[0, k], sem.at[1, k], dev)

        copies = [
            cp(y, lo, 0, dev_up), cp(y, hi, 1, dev_down), cp(y, hi, 2, dev_up), cp(y, lo, 3, dev_down),
            cp(down, lo, 4, dev_up), cp(up, hi, 5, dev_down),
        ]
        for k in range(4):
            started(f"{name}{k}", copies[k])
        return copies

    def gather_forward(name, copies):
        wait(f"{name}0")
        started(f"{name}4", copies[4])
        wait(f"{name}1")
        started(f"{name}5", copies[5])

    def wait_halo(k):
        for h in range(HALVES):
            wait(f"halo{h}{k}")

    def local_tab(r):
        tab[r, 0:N, :] = dot(feat[...], w[r]).astype(BF16)

    def slot_rows(slot):
        return pl.ds(pl.multiple_of(slot * S, S), S)

    def turn_halo(slot):
        tabT[slot_rows(slot), N:T] = jnp.transpose(halo[slot], (1, 0))

    gathers = {}

    def gather_halo(h):
        wait(f"slabs{h}")
        gathers[h] = gather_start(f"halo{h}", halo, part_cols[h], ag1_sem.at[h])

    loop(R, counts)
    wait("feat")
    gather_halo(0)
    loop(R, local_tab)
    share_weights()
    gather_halo(1)
    gather_forward("halo0", gathers[0])

    local = dot(feat[...], w[R])
    for r in range(R):
        local = local + dot(cnt[r, :, 0:N], tab[r, 0:N, :])
    pre[...] = local
    gather_forward("halo1", gathers[1])

    def own_tab(r):
        tacc[r] = dot(halo[y], w[r, slot_rows(y), :])

    def near_tab(r):
        tacc[r] += dot(halo[down], w[r, slot_rows(down), :]) + dot(halo[up], w[r, slot_rows(up), :])

    loop(R, own_tab)
    tabT[:, 0:N] = jnp.transpose(feat[...], (1, 0))
    turn_halo(y)
    wait_halo(2)
    wait_halo(3)
    loop(R, near_tab)
    turn_halo(down)
    turn_halo(up)
    wait_halo(4)
    wait_halo(5)

    def far_tab(r):
        tab[r, N:T, :] = (tacc[r] + dot(halo[far], w[r, slot_rows(far), :])).astype(BF16)

    for r in range(R):
        far_tab(r)
    total = pre[...]
    for r in range(R):
        total = total + dot(cnt[r, :, N:T], tab[r, N:T, :])
    pre[...] = total

    wait("cot")
    tile = min(128, N)

    def activate(i):
        rows = pl.ds(pl.multiple_of(i * tile, tile), tile)
        v = pre[rows, :]
        s = 1.0 / (1.0 + jnp.exp(-v))
        out[rows, :] = (v * s).astype(BF16)
        dp[y, rows, :] = (cot[rows, :].astype(F32) * (s * (1.0 + v * (1.0 - s)))).astype(BF16)

    loop(N // tile, activate)
    ag2 = [
        remote(dp.at[slot, rows, :], dp.at[slot, rows, :], ag2_sem.at[0, k], ag2_sem.at[1, k], at(q, c, to))
        for k, (slot, first, count, to) in enumerate((
            (y, 0, 1, up), (y, 2, 1, down), (y, 1, 1, up), (y, 3, 1, down), (y, 2, 2, up), (y, 0, 2, down),
            (down, 0, 1, up), (up, 2, 1, down), (down, 1, 1, up), (up, 3, 1, down),
        ))
        for rows in [pl.ds(first * (N // 4), count * (N // 4))]
    ]
    for k in range(6):
        started(f"dp{k}", ag2[k])

    def forward_dp(k):
        wait(f"dp{k}")
        started(f"dp{k + 6}", ag2[k + 6])

    dT[...] = jnp.transpose(dp[y], (1, 0))
    turn_halo(far)

    def core_copy(p):
        return remote(gsend.at[p], grecv.at[p], gc_sem.at[0, p], gc_sem.at[1, p], sibling)

    def put_terms(p, part):
        part = part.reshape(CH, CORES, GR, O)
        gown[p] = jnp.where(c == 0, part[:, 0], part[:, 1])
        gsend[p] = jnp.where(c == 0, part[:, 1], part[:, 0]).astype(BF16)
        started(f"core{p}", core_copy(p))

    def relation_terms(r):
        eT[r] = dot(dT[...], cnt[r]).astype(BF16)
        put_terms(r + 1, dot_nt(tabT[...], eT[r]))

    x_up, x_down, x_far = ring(x + 1, X), ring(x - 1, X), ring(x + 2, X)
    zh = Z // 2

    def x_copy(p, k, block, to):
        return remote(block, rx.at[p, k], gx_sem.at[0, p, k], gx_sem.at[1, p, k], at(to * Z + z, c, y))

    def far_x(p):
        wait(f"core{p}")
        some = min(8, CH)

        def body(i):
            chips = pl.ds(i * some, some)
            total = gown[p, chips] + grecv[p, chips].astype(F32)
            gown[p, chips] = total
            gx[p, chips] = total.astype(BF16)

        loop(CH // some, body)
        for k, to in enumerate((x_up, x_down)):
            block = gx.at[p, pl.ds(x_far * Z + k * zh, zh)]
            sems = gr_sem.at[0, p, k], gr_sem.at[1, p, k]
            started(f"r{p}{k}", remote(block, relay.at[p, k], *sems, at(to * Z + z, c, y)))

    def near_x(p):
        for k, to in enumerate((x_up, x_down)):
            wait(f"r{p}{k}")
            part = pl.ds(to * Z + k * zh, zh)
            gx[p, part] = (gown[p, part] + relay[p, k].astype(F32)).astype(BF16)
            started(f"x{p}{k}", x_copy(p, k, gx.at[p, pl.ds(to * Z, Z)], to))

    def far_z():
        wait(f"core{R}")

        def body(i):
            chips = pl.ds(i * Z, Z)
            total = gown[R, chips] + grecv[R, chips].astype(F32)
            gown[R, chips] = total
            lz[i] = total.astype(BF16)

        loop(X, body)
        for k in range(1, Z):
            to = ring(z + k, Z)
            sems = lz_sem.at[0, k], lz_sem.at[1, k]
            started(f"lz{k}", remote(lz.at[:, to], lzr.at[k - 1], *sems, at(x * Z + to, c, y)))

    def near_z():
        for k in range(1, Z):
            wait(f"lz{k}")

        def body(i):
            total = gown[R, i * Z + z]
            for k in range(1, Z):
                total = total + lzr[k - 1, i].astype(F32)
            lsum[i] = total
            lx[i] = total.astype(BF16)

        loop(X, body)
        for k in range(1, X):
            to = ring(x + k, X)
            sems = lx_sem.at[0, k], lx_sem.at[1, k]
            started(f"lx{k}", remote(lx.at[to], lxr.at[k - 1], *sems, at(to * Z + z, c, y)))

    put_terms(0, dot(tabT[:, 0:N], dp[y]))
    for r in range(R):
        relation_terms(r)
        far_x(r)
    forward_dp(0)
    forward_dp(1)
    far_z()
    forward_dp(2)
    forward_dp(3)
    pass_weights()

    def own_back(r):
        bacc[r] = dot_nt(w[r, slot_rows(y), :], dp[y])

    def near_back(r):
        bacc[r] += dot_nt(wd[0, r], dp[down]) + dot_nt(wd[2, r], dp[up])

    def far_back(r):
        bT[r] = (bacc[r] + dot_nt(wd[1, r], dp[far])).astype(BF16)

    near_x(0)
    loop(R + 1, own_back)
    for p in range(1, R):
        near_x(p)
    wait("wf")
    for k in (4, 5):
        wait(f"dp{k}")
    loop(R + 1, near_back)
    for k in (6, 7, 8, 9):
        wait(f"dp{k}")
    for r in range(R):
        far_back(r)
    received = dot(bT[0], cnt[0, :, N:T])
    for r in range(1, R):
        received = received + dot(bT[r], cnt[r, :, N:T])

    hg[...] = jnp.transpose(received, (1, 0)).astype(BF16)
    ret[mine, :] = hg[mine, :]

    def return_slab(i):
        chip, rows = chip_rows(i)
        remote(hg.at[rows, :], ret.at[mine, :], ret_sem.at[0], ret_sem.at[1], at(chip, c, y)).start()

    loop(CH - 1, return_slab)
    ret_all = remote(hg.at[others, :], ret.at[others, :], ret_sem.at[0], ret_sem.at[1], sibling)
    pending["ret"] = ret_all.wait_recv
    pending["ret out"] = ret_all.wait_send

    def z_copy(g, places, k):
        to = ring(z + k, Z)
        return remote(
            gzs.at[places, to], rz.at[k - 1, places], gz_sem.at[0, g, k], gz_sem.at[1, g, k], at(x * Z + to, c, y)
        )

    def along_z(g, first, last):
        for p in range(first, last):
            total = gown[p, pl.ds(x * Z, Z)]
            for k in range(2):
                wait(f"x{p}{k}")
                total = total + rx[p, k].astype(F32)
            gz[p] = total
            gzs[p] = total.astype(BF16)
        for k in range(1, Z):
            started(f"z{g}{k}", z_copy(g, pl.ds(first, last - first), k))

    first_group = R // 2
    along_z(0, 0, first_group)

    own = bacc[R] + dot_nt(wd[1, R], dp[far])
    for r in range(R):
        own = own + dot(bT[r], cnt[r, :, 0:N])
    grad[...] = jnp.transpose(own, (1, 0))

    def owner_map(k):
        rows = lax.broadcasted_iota(jnp.int32, (N, HR), 0)
        named = jnp.transpose(jnp.broadcast_to(sendcol[k], (HR, 8)), (1, 0))[0:1]
        return jnp.where(named == rows, 1.0, 0.0).astype(BF16)

    for k in range(2):
        owners[k] = owner_map(k)
    near_z()
    along_z(1, first_group, R)

    wait("ret")
    started("rets", remote(ret, rets, rsib_sem.at[0], rsib_sem.at[1], sibling))
    grad[...] += dot(owners[0], ret[...])
    wait("rets")
    gf[...] = (grad[...] + dot(owners[1], rets[...])).astype(BF16)

    def total_terms(p, r):
        total = gz[p, z]
        for k in range(1, Z):
            total = total + rz[k - 1, p].astype(F32)
        gw[r] = total

    for k in range(1, Z):
        wait(f"z0{k}")
        wait(f"z1{k}")
    total_terms(0, R)
    loop(R - 1, lambda r: total_terms(r + 1, r))
    last = lsum[x]
    for k in range(1, X):
        wait(f"lx{k}")
        last = last + lxr[k - 1].astype(F32)
    gw[R - 1] = last
    finish()


def hand_out(*refs):
    for here, there in zip(refs[:3], refs[3:]):
        there[...] = here[...]


def shards(X, Z, features, history, weights, cotangent, send_rows, neighbors):
    N, D = features.shape
    R, _, K = neighbors.shape
    O = weights.shape[2]
    Y = lax.axis_size("mp")
    S = D // Y
    CH = X * Z
    SL = CORES * send_rows.shape[2]
    HR = CH * SL
    T = N + HR
    GR = D // (CH * CORES)

    dma = pltpu.SemaphoreType.DMA
    vmem = pl.BlockSpec(memory_space=pltpu.VMEM)
    anywhere = pl.BlockSpec(memory_space=pl.ANY)
    results = pl.pallas_call(
        functools.partial(kernel, X, Z, Y),
        out_shape=(
            jax.ShapeDtypeStruct((N, O), BF16),
            jax.ShapeDtypeStruct((N, S), BF16),
            jax.ShapeDtypeStruct((R + 1, GR, O), F32),
        ),
        in_specs=[anywhere] * 6,
        out_specs=(vmem, vmem, vmem),
        scratch_shapes=[
            pltpu.VMEM((N, D), BF16),
            pltpu.VMEM((R + 1, D, O), BF16),
            pltpu.VMEM((N, O), BF16),
            pltpu.VMEM((R, K, N), jnp.int32),
            pltpu.VMEM((SL // CORES, CH * CORES), jnp.int32),
            pltpu.VMEM((CH * CORES, SL // CORES), F32),
            pltpu.VMEM((2, HR, 1), jnp.int32),
            pltpu.VMEM((N, S), F32),
            pltpu.VMEM((2 * N, S), BF16),
            pltpu.VMEM((HR, S), BF16),
            pltpu.VMEM((HR, S), BF16),
            pltpu.VMEM((HR, S), BF16),
            pltpu.VMEM((HR, S), BF16),
            pltpu.VMEM((Y, HR, S), BF16),
            pltpu.VMEM((Y - 1, R + 1, S, O), BF16),
            pltpu.VMEM((R, N, K), jnp.int32),
            pltpu.VMEM((R, N, T), BF16),
            pltpu.VMEM((R, T, O), BF16),
            pltpu.VMEM((R, HR, O), F32),
            pltpu.VMEM((N, O), F32),
            pltpu.VMEM((D, T), BF16),
            pltpu.VMEM((Y, N, O), BF16),
            pltpu.VMEM((O, N), BF16),
            pltpu.VMEM((R, O, T), BF16),
            pltpu.VMEM((R + 1, S, N), F32),
            pltpu.VMEM((R + 1, CH, GR, O), BF16),
            pltpu.VMEM((R + 1, CH, GR, O), F32),
            pltpu.VMEM((R + 1, CH, GR, O), BF16),
            pltpu.VMEM((R, CH, GR, O), BF16),
            pltpu.VMEM((R, 2, Z // 2, GR, O), BF16),
            pltpu.VMEM((R, 2, Z, GR, O), BF16),
            pltpu.VMEM((R, Z, GR, O), F32),
            pltpu.VMEM((R, Z, GR, O), BF16),
            pltpu.VMEM((Z - 1, R, GR, O), BF16),
            pltpu.VMEM((X, Z, GR, O), BF16),
            pltpu.VMEM((Z - 1, X, GR, O), BF16),
            pltpu.VMEM((X, GR, O), F32),
            pltpu.VMEM((X, GR, O), BF16),
            pltpu.VMEM((X - 1, GR, O), BF16),
            pltpu.VMEM((R, S, N), BF16),
            pltpu.VMEM((N, S), F32),
            pltpu.VMEM((2, N, HR), BF16),
            pltpu.VMEM((HR, S), BF16),
            pltpu.VMEM((HR, S), BF16),
            pltpu.VMEM((HR, S), BF16),
            dma((7,)),
            dma((2,)),
            dma((2, HALVES)),
            dma((2, Y)),
            dma((2, X)),
            dma((2,)),
            dma((HALVES, 2, 6)),
            dma((2, 10)),
            dma((2, R + 1)),
            dma((2, R, 2)),
            dma((2, R, 2)),
            dma((2, 2, Z)),
            dma((2, Z)),
            dma((2, X)),
            dma((2,)),
            dma((2,)),
        ],
        compiler_params=pltpu.CompilerParams(
            collective_id=0, has_side_effects=True, vmem_limit_bytes=58 * 1024 * 1024
        ),
        name="graph_layer",
    )(
        features,
        history,
        jnp.transpose(weights, (1, 0, 2)),
        cotangent,
        jnp.transpose(send_rows[0], (1, 0)),
        jnp.transpose(neighbors, (0, 2, 1)),
    )
    out, gf, gw = pl.pallas_call(
        hand_out,
        out_shape=tuple(jax.ShapeDtypeStruct(one.shape, one.dtype) for one in results),
        in_specs=[vmem] * 3,
        out_specs=(vmem,) * 3,
        name="hand_out",
    )(*results)
    return out, gf, jnp.transpose(gw, (1, 0, 2))


def solution(mesh):
    in_specs = (
        P("dom", None),
        P("dom", None),
        P(None, None, "mp"),
        P("dom", "mp"),
        P("dom", None, None),
        P(None, "dom", None),
    )
    out_specs = (P("dom", "mp"), P("dom", "mp"), P("dom", None, "mp"))
    chips = mesh.shape["dom"] // CORES
    X = 4 if chips >= 8 else 2
    return jax.shard_map(
        functools.partial(shards, X, chips // X), mesh=mesh, in_specs=in_specs, out_specs=out_specs, check_vma=False
    )
```

```python
import functools

import jax
import jax.numpy as jnp
from jax import lax
from jax.experimental import pallas as pl
from jax.experimental.pallas import tpu as pltpu
from jax.sharding import PartitionSpec as P

MESH = pl.DeviceIdType.MESH
CORES = 2
HALVES = 2
F32 = jnp.float32
BF16 = jnp.bfloat16


def dot(a, b):
    return jnp.dot(a, b, preferred_element_type=F32)


def dot_nt(a, b):
    return lax.dot_general(a, b, (((1,), (1,)), ((), ())), preferred_element_type=F32)


def loop(count, body):
    lax.fori_loop(0, count, lambda i, c: (body(i), c)[1], 0)


def kernel(
    X, Z, Y,
    feat_in, hist_in, w_in, cot_in, send_in, nbr_in,
    out, gf, gw,
    feat, w, cot, nbr, sendT, tcol, sendcol, histv, src, asib, aown, arecv, slabs, halo, wd, nbrcol, cnt, tab, tacc, pre, tabT,
    dp, dT, eT, bacc, gsend, gown, grecv, gx, relay, rx, gz, gzs, rz, lz, lzr, lsum, lx, lxr, bT, grad, owners, hg, ret, rets,
    in_sem, sib_sem, halo_sem, w_sem, wx_sem, wf_sem, ag1_sem, ag2_sem, gc_sem, gr_sem, gx_sem, gz_sem, lz_sem, lx_sem, ret_sem, rsib_sem,
):
    N, D = feat.shape
    R = nbr.shape[0]
    K = nbr.shape[1]
    O = w.shape[2]
    S = D // Y
    CH = X * Z
    HR = halo.shape[1]
    SL = HR // CH
    T = N + HR
    GR = gw.shape[1]
    SEND = SL // CORES

    dom = lax.axis_index("dom")
    y = lax.axis_index("mp")
    c = lax.rem(dom, CORES)
    q = dom // CORES
    z = lax.rem(q, Z)
    x = q // Z

    def at(chip, core, yy):
        return {"dom": chip * CORES + core, "mp": yy}

    def ring(v, size):
        return lax.rem(v + size, size)

    def remote(s, d, ss, rs, dev):
        return pltpu.make_async_remote_copy(
            src_ref=s, dst_ref=d, send_sem=ss, recv_sem=rs, device_id=dev, device_id_type=MESH
        )

    sibling = at(q, 1 - c, y)
    up, down, far = ring(y + 1, Y), ring(y - 1, Y), ring(y + 2, Y)

    pending = {}

    def wait(name):
        pending.pop(name)()

    def started(name, copy):
        copy.start()
        pending[name] = copy.wait_recv
        pending[name + " out"] = copy.wait_send
        return copy

    def finish():
        for one in list(pending):
            wait(one)

    columns = pl.ds(pl.multiple_of(y * S, 128), S)
    inputs = [
        ("send", send_in, sendT),
        ("feat slice", feat_in.at[:, columns], src.at[pl.ds(0, N), :]),
        ("hist", hist_in.at[:, columns], histv),
        ("w", w_in, w),
        ("nbr", nbr_in, nbr),
        ("feat", feat_in, feat),
        ("cot", cot_in, cot),
    ]

    def fetch(first, last):
        for i in range(first, last):
            name, here, there = inputs[i]
            cp = pltpu.make_async_copy(here, there, in_sem.at[i])
            cp.start()
            pending[name] = cp.wait

    fetch(0, 3)

    barrier = pltpu.get_barrier_semaphore()

    def greet(dev):
        pl.semaphore_signal(barrier, inc=1, device_id=dev, device_id_type=MESH)

    greet(sibling)
    for k in range(1, Y):
        greet(at(q, c, ring(y + k, Y)))
    loop(CH - 1, lambda i: greet(at(lax.rem(q + 1 + i, CH), c, y)))

    wait("send")
    tcol[...] = jnp.transpose(sendT[...].astype(F32), (1, 0))
    even, odd = tcol[pl.ds(0, CH, stride=2), :], tcol[pl.ds(1, CH, stride=2), :]
    slot = lax.broadcasted_iota(jnp.int32, (CH, SL, SEND), 1)
    lane = lax.broadcasted_iota(jnp.int32, (CH, SL, SEND), 2)
    taken = slot == lane + c * SEND
    for k, rows in enumerate((jnp.where(c == 0, even, odd), jnp.where(c == 0, odd, even))):
        wide = jnp.broadcast_to(rows[:, None, :], (CH, SL, SEND))
        found = jnp.sum(jnp.where(taken, wide + 1.0, 0.0), axis=2, keepdims=True) - 1.0
        sendcol[k] = found.reshape(HR, 1).astype(jnp.int32)
    wait("feat slice")
    wait("hist")
    fetch(3, len(inputs))
    src[N : 2 * N, :] = histv[...].astype(BF16)

    def pick(k, dst):
        step = min(256, HR)

        def body(i):
            rows = pl.ds(i * step, step)
            col = jnp.broadcast_to(sendcol[k, rows, :].astype(jnp.int16), (step, 2 * N))
            named = col == lax.broadcasted_iota(jnp.int16, (step, 2 * N), 1)
            sel = jnp.where(named, jnp.asarray(1.0, BF16), jnp.asarray(0.0, BF16))
            dst[rows, :] = dot(sel, src[...]).astype(BF16)

        for i in range(HR // step):
            body(i)

    pick(1, asib)
    pl.semaphore_wait(barrier, CH + Y - 1)

    half = S // CORES
    piece = half // X
    half_rows = pl.ds(pl.multiple_of(c * half, half), half)
    piece_rows = pl.ds(pl.multiple_of(c * half + x * piece, piece), piece)

    def send_weights(k):
        to = ring(y + k, Y)
        rows = pl.ds(pl.multiple_of(to * S + c * half + x * piece, piece), piece)
        sems = w_sem.at[0, k], w_sem.at[1, k]
        started(f"w{k}", remote(w.at[:, rows, :], wd.at[k - 1, :, piece_rows, :], *sems, at(q, c, to)))

    def share_weights():
        for k in range(1, Y):
            wait(f"w{k}")
        part = wd.at[:, :, piece_rows, :]
        for k in range(1, X):
            to = at(ring(x + k, X) * Z + z, c, y)
            started(f"wx{k}", remote(part, part, wx_sem.at[0, k], wx_sem.at[1, k], to))

    def pass_weights():
        for k in range(1, X):
            wait(f"wx{k}")
        part = wd.at[:, :, half_rows, :]
        started("wf", remote(part, part, wf_sem.at[0], wf_sem.at[1], sibling))

    started("sib", remote(asib, arecv, sib_sem.at[0], sib_sem.at[1], sibling))
    pick(0, aown)
    wait("sib")
    slabs[...] = aown[...] + arecv[...]
    mine = pl.ds(pl.multiple_of(q * SL, SL), SL)
    halo[y, mine, :] = slabs[mine, :]

    def other_chips(body):
        for dz in sorted(range(Z), key=lambda d: -min(d, Z - d)):

            def along(i):
                chip = ring(x + X // 2 + i, X) * Z + ring(z + dz, Z)
                body(chip, pl.ds(pl.multiple_of(chip * SL, SL), SL))

            if dz:
                loop(X, along)
            else:
                for i in range(X):
                    if i != X // 2:
                        along(i)

    others = pl.ds(0, HR - SL)
    part_cols = [pl.ds(h * (S // HALVES), S // HALVES) for h in range(HALVES)]
    for h, cols in enumerate(part_cols):
        sems = halo_sem.at[0, h], halo_sem.at[1, h]

        def send_slab(chip, rows):
            remote(slabs.at[rows, cols], halo.at[y, mine, cols], *sems, at(chip, c, y)).start()

        other_chips(send_slab)
        everything = remote(slabs.at[others, cols], halo.at[y, others, cols], *sems, sibling)
        pending[f"slabs{h}"] = everything.wait_recv
        pending[f"slabs{h} out"] = everything.wait_send

    wait("w")
    for k in (2, 1, 3):
        send_weights(k)

    wait("nbr")

    def counts(r):
        nbrcol[r] = jnp.transpose(nbr[r], (1, 0))
        step = min(128, N)
        share, none = jnp.asarray(1.0 / K, BF16), jnp.asarray(0.0, BF16)

        def body(i):
            rows = pl.ds(pl.multiple_of(i * step, step), step)
            cols = nbrcol[r, rows, :].astype(jnp.int16)
            pos = lax.broadcasted_iota(jnp.int16, (step, T), 1)
            total = jnp.zeros((step, T), BF16)
            for k in range(K):
                total = total + jnp.where(jnp.broadcast_to(cols[:, k : k + 1], (step, T)) == pos, share, none)
            cnt[r, rows, :] = total

        loop(N // step, body)

    def gather_start(name, buf, cols, sem):
        m = buf.shape[1] // 2
        lo, hi = pl.ds(0, m), pl.ds(m, m)
        dev_up, dev_down = at(q, c, up), at(q, c, down)

        def cp(slot, rows, k, dev):
            part = buf.at[slot, rows, cols]
            return remote(part, part, sem.at[0, k], sem.at[1, k], dev)

        copies = [
            cp(y, lo, 0, dev_up), cp(y, hi, 1, dev_down), cp(y, hi, 2, dev_up), cp(y, lo, 3, dev_down),
            cp(down, lo, 4, dev_up), cp(up, hi, 5, dev_down),
        ]
        for k in range(4):
            started(f"{name}{k}", copies[k])
        return copies

    def gather_forward(name, copies):
        wait(f"{name}0")
        started(f"{name}4", copies[4])
        wait(f"{name}1")
        started(f"{name}5", copies[5])

    def wait_halo(k):
        for h in range(HALVES):
            wait(f"halo{h}{k}")

    def local_tab(r):
        tab[r, 0:N, :] = dot(feat[...], w[r]).astype(BF16)

    def slot_rows(slot):
        return pl.ds(pl.multiple_of(slot * S, S), S)

    def turn_halo(slot):
        tabT[slot_rows(slot), N:T] = jnp.transpose(halo[slot], (1, 0))

    gathers = {}

    def gather_halo(h):
        wait(f"slabs{h}")
        gathers[h] = gather_start(f"halo{h}", halo, part_cols[h], ag1_sem.at[h])

    loop(R, counts)
    wait("feat")
    gather_halo(0)
    loop(R, local_tab)
    share_weights()
    gather_halo(1)
    gather_forward("halo0", gathers[0])

    local = dot(feat[...], w[R])
    for r in range(R):
        local = local + dot(cnt[r, :, 0:N], tab[r, 0:N, :])
    pre[...] = local
    gather_forward("halo1", gathers[1])

    def own_tab(r):
        tacc[r] = dot(halo[y], w[r, slot_rows(y), :])

    def near_tab(r):
        tacc[r] += dot(halo[down], w[r, slot_rows(down), :]) + dot(halo[up], w[r, slot_rows(up), :])

    loop(R, own_tab)
    tabT[:, 0:N] = jnp.transpose(feat[...], (1, 0))
    turn_halo(y)
    wait_halo(2)
    wait_halo(3)
    loop(R, near_tab)
    turn_halo(down)
    turn_halo(up)
    wait_halo(4)
    wait_halo(5)

    def far_tab(r):
        tab[r, N:T, :] = (tacc[r] + dot(halo[far], w[r, slot_rows(far), :])).astype(BF16)

    for r in range(R):
        far_tab(r)
    total = pre[...]
    for r in range(R):
        total = total + dot(cnt[r, :, N:T], tab[r, N:T, :])
    pre[...] = total

    wait("cot")
    tile = min(128, N)

    def activate(i):
        rows = pl.ds(pl.multiple_of(i * tile, tile), tile)
        v = pre[rows, :]
        s = 1.0 / (1.0 + jnp.exp(-v))
        out[rows, :] = (v * s).astype(BF16)
        dp[y, rows, :] = (cot[rows, :].astype(F32) * (s * (1.0 + v * (1.0 - s)))).astype(BF16)

    loop(N // tile, activate)
    ag2 = [
        remote(dp.at[slot, rows, :], dp.at[slot, rows, :], ag2_sem.at[0, k], ag2_sem.at[1, k], at(q, c, to))
        for k, (slot, first, count, to) in enumerate((
            (y, 0, 1, up), (y, 2, 1, down), (y, 1, 1, up), (y, 3, 1, down), (y, 2, 2, up), (y, 0, 2, down),
            (down, 0, 1, up), (up, 2, 1, down), (down, 1, 1, up), (up, 3, 1, down),
        ))
        for rows in [pl.ds(first * (N // 4), count * (N // 4))]
    ]
    for k in range(6):
        started(f"dp{k}", ag2[k])

    def forward_dp(k):
        wait(f"dp{k}")
        started(f"dp{k + 6}", ag2[k + 6])

    dT[...] = jnp.transpose(dp[y], (1, 0))
    turn_halo(far)

    def core_copy(p):
        return remote(gsend.at[p], grecv.at[p], gc_sem.at[0, p], gc_sem.at[1, p], sibling)

    def put_terms(p, part):
        part = part.reshape(CH, CORES, GR, O)
        gown[p] = jnp.where(c == 0, part[:, 0], part[:, 1])
        gsend[p] = jnp.where(c == 0, part[:, 1], part[:, 0]).astype(BF16)
        started(f"core{p}", core_copy(p))

    def relation_terms(r):
        eT[r] = dot(dT[...], cnt[r]).astype(BF16)
        put_terms(r + 1, dot_nt(tabT[...], eT[r]))

    x_up, x_down, x_far = ring(x + 1, X), ring(x - 1, X), ring(x + 2, X)
    zh = Z // 2

    def x_copy(p, k, block, to):
        return remote(block, rx.at[p, k], gx_sem.at[0, p, k], gx_sem.at[1, p, k], at(to * Z + z, c, y))

    def far_x(p):
        wait(f"core{p}")
        some = min(8, CH)

        def body(i):
            chips = pl.ds(i * some, some)
            total = gown[p, chips] + grecv[p, chips].astype(F32)
            gown[p, chips] = total
            gx[p, chips] = total.astype(BF16)

        loop(CH // some, body)
        for k, to in enumerate((x_up, x_down)):
            block = gx.at[p, pl.ds(x_far * Z + k * zh, zh)]
            sems = gr_sem.at[0, p, k], gr_sem.at[1, p, k]
            started(f"r{p}{k}", remote(block, relay.at[p, k], *sems, at(to * Z + z, c, y)))

    def near_x(p):
        for k, to in enumerate((x_up, x_down)):
            wait(f"r{p}{k}")
            part = pl.ds(to * Z + k * zh, zh)
            gx[p, part] = (gown[p, part] + relay[p, k].astype(F32)).astype(BF16)
            started(f"x{p}{k}", x_copy(p, k, gx.at[p, pl.ds(to * Z, Z)], to))

    z_first = (0, R)

    def far_z(l):
        p = z_first[l]
        wait(f"core{p}")

        def body(i):
            chips = pl.ds(i * Z, Z)
            total = gown[p, chips] + grecv[p, chips].astype(F32)
            gown[p, chips] = total
            lz[l, i] = total.astype(BF16)

        loop(X, body)
        for k in range(1, Z):
            to = ring(z + k, Z)
            sems = lz_sem.at[l, 0, k], lz_sem.at[l, 1, k]
            started(f"lz{l}{k}", remote(lz.at[l, :, to], lzr.at[l, k - 1], *sems, at(x * Z + to, c, y)))

    def near_z(l):
        for k in range(1, Z):
            wait(f"lz{l}{k}")

        def body(i):
            total = gown[z_first[l], i * Z + z]
            for k in range(1, Z):
                total = total + lzr[l, k - 1, i].astype(F32)
            lsum[l, i] = total
            lx[l, i] = total.astype(BF16)

        loop(X, body)
        for k in range(1, X):
            to = ring(x + k, X)
            sems = lx_sem.at[l, 0, k], lx_sem.at[l, 1, k]
            started(f"lx{l}{k}", remote(lx.at[l, to], lxr.at[l, k - 1], *sems, at(to * Z + z, c, y)))

    put_terms(0, dot(tabT[:, 0:N], dp[y]))
    relation_terms(0)
    far_z(0)
    for r in range(1, R):
        relation_terms(r)
        far_x(r)
        if r == R - 2:
            forward_dp(0)
            forward_dp(1)
    forward_dp(2)
    forward_dp(3)
    far_z(1)
    pass_weights()

    def own_back(r):
        bacc[r] = dot_nt(w[r, slot_rows(y), :], dp[y])

    def near_back(r):
        bacc[r] += dot_nt(wd[0, r], dp[down]) + dot_nt(wd[2, r], dp[up])

    def far_back(r):
        bT[r] = (bacc[r] + dot_nt(wd[1, r], dp[far])).astype(BF16)

    loop(R + 1, own_back)
    for p in range(1, R):
        near_x(p)
    wait("wf")
    for k in (4, 5):
        wait(f"dp{k}")
    loop(R + 1, near_back)
    for k in (6, 7, 8, 9):
        wait(f"dp{k}")
    for r in range(R):
        far_back(r)
    received = dot(bT[0], cnt[0, :, N:T])
    for r in range(1, R):
        received = received + dot(bT[r], cnt[r, :, N:T])

    hg[...] = jnp.transpose(received, (1, 0)).astype(BF16)
    ret[mine, :] = hg[mine, :]

    def return_slab(chip, rows):
        remote(hg.at[rows, :], ret.at[mine, :], ret_sem.at[0], ret_sem.at[1], at(chip, c, y)).start()

    other_chips(return_slab)
    ret_all = remote(hg.at[others, :], ret.at[others, :], ret_sem.at[0], ret_sem.at[1], sibling)
    pending["ret"] = ret_all.wait_recv
    pending["ret out"] = ret_all.wait_send

    def z_copy(g, places, k):
        to = ring(z + k, Z)
        return remote(
            gzs.at[places, to], rz.at[k - 1, places], gz_sem.at[0, g, k], gz_sem.at[1, g, k], at(x * Z + to, c, y)
        )

    def along_z(g, first, last):
        for p in range(first, last):
            total = gown[p, pl.ds(x * Z, Z)]
            for k in range(2):
                wait(f"x{p}{k}")
                total = total + rx[p, k].astype(F32)
            gz[p] = total
            gzs[p] = total.astype(BF16)
        for k in range(1, Z):
            started(f"z{g}{k}", z_copy(g, pl.ds(first, last - first), k))

    near_z(0)
    along_z(0, 1, R - 1)

    own = bacc[R] + dot_nt(wd[1, R], dp[far])
    for r in range(R):
        own = own + dot(bT[r], cnt[r, :, 0:N])
    grad[...] = jnp.transpose(own, (1, 0))

    def owner_map(k):
        rows = lax.broadcasted_iota(jnp.int32, (N, HR), 0)
        named = jnp.transpose(jnp.broadcast_to(sendcol[k], (HR, 8)), (1, 0))[0:1]
        return jnp.where(named == rows, 1.0, 0.0).astype(BF16)

    for k in range(2):
        owners[k] = owner_map(k)
    near_z(1)
    along_z(1, R - 1, R)

    wait("ret")
    started("rets", remote(ret, rets, rsib_sem.at[0], rsib_sem.at[1], sibling))
    grad[...] += dot(owners[0], ret[...])
    wait("rets")
    gf[...] = (grad[...] + dot(owners[1], rets[...])).astype(BF16)

    def total_terms(p, r):
        total = gz[p, z]
        for k in range(1, Z):
            total = total + rz[k - 1, p].astype(F32)
        gw[r] = total

    for k in range(1, Z):
        wait(f"z0{k}")
        wait(f"z1{k}")
    loop(R - 1, lambda r: total_terms(r + 1, r))
    for l, r in enumerate((R, R - 1)):
        last = lsum[l, x]
        for k in range(1, X):
            wait(f"lx{l}{k}")
            last = last + lxr[l, k - 1].astype(F32)
        gw[r] = last
    finish()


def hand_out(*refs):
    for here, there in zip(refs[:3], refs[3:]):
        there[...] = here[...]


def shards(X, Z, features, history, weights, cotangent, send_rows, neighbors):
    N, D = features.shape
    R, _, K = neighbors.shape
    O = weights.shape[2]
    Y = lax.axis_size("mp")
    S = D // Y
    CH = X * Z
    SL = CORES * send_rows.shape[2]
    HR = CH * SL
    T = N + HR
    GR = D // (CH * CORES)

    dma = pltpu.SemaphoreType.DMA
    vmem = pl.BlockSpec(memory_space=pltpu.VMEM)
    anywhere = pl.BlockSpec(memory_space=pl.ANY)
    results = pl.pallas_call(
        functools.partial(kernel, X, Z, Y),
        out_shape=(
            jax.ShapeDtypeStruct((N, O), BF16),
            jax.ShapeDtypeStruct((N, S), BF16),
            jax.ShapeDtypeStruct((R + 1, GR, O), F32),
        ),
        in_specs=[anywhere] * 6,
        out_specs=(vmem, vmem, vmem),
        scratch_shapes=[
            pltpu.VMEM((N, D), BF16),
            pltpu.VMEM((R + 1, D, O), BF16),
            pltpu.VMEM((N, O), BF16),
            pltpu.VMEM((R, K, N), jnp.int32),
            pltpu.VMEM((SL // CORES, CH * CORES), jnp.int32),
            pltpu.VMEM((CH * CORES, SL // CORES), F32),
            pltpu.VMEM((2, HR, 1), jnp.int32),
            pltpu.VMEM((N, S), F32),
            pltpu.VMEM((2 * N, S), BF16),
            pltpu.VMEM((HR, S), BF16),
            pltpu.VMEM((HR, S), BF16),
            pltpu.VMEM((HR, S), BF16),
            pltpu.VMEM((HR, S), BF16),
            pltpu.VMEM((Y, HR, S), BF16),
            pltpu.VMEM((Y - 1, R + 1, S, O), BF16),
            pltpu.VMEM((R, N, K), jnp.int32),
            pltpu.VMEM((R, N, T), BF16),
            pltpu.VMEM((R, T, O), BF16),
            pltpu.VMEM((R, HR, O), F32),
            pltpu.VMEM((N, O), F32),
            pltpu.VMEM((D, T), BF16),
            pltpu.VMEM((Y, N, O), BF16),
            pltpu.VMEM((O, N), BF16),
            pltpu.VMEM((R, O, T), BF16),
            pltpu.VMEM((R + 1, S, N), F32),
            pltpu.VMEM((R + 1, CH, GR, O), BF16),
            pltpu.VMEM((R + 1, CH, GR, O), F32),
            pltpu.VMEM((R + 1, CH, GR, O), BF16),
            pltpu.VMEM((R, CH, GR, O), BF16),
            pltpu.VMEM((R, 2, Z // 2, GR, O), BF16),
            pltpu.VMEM((R, 2, Z, GR, O), BF16),
            pltpu.VMEM((R, Z, GR, O), F32),
            pltpu.VMEM((R, Z, GR, O), BF16),
            pltpu.VMEM((Z - 1, R, GR, O), BF16),
            pltpu.VMEM((2, X, Z, GR, O), BF16),
            pltpu.VMEM((2, Z - 1, X, GR, O), BF16),
            pltpu.VMEM((2, X, GR, O), F32),
            pltpu.VMEM((2, X, GR, O), BF16),
            pltpu.VMEM((2, X - 1, GR, O), BF16),
            pltpu.VMEM((R, S, N), BF16),
            pltpu.VMEM((N, S), F32),
            pltpu.VMEM((2, N, HR), BF16),
            pltpu.VMEM((HR, S), BF16),
            pltpu.VMEM((HR, S), BF16),
            pltpu.VMEM((HR, S), BF16),
            dma((7,)),
            dma((2,)),
            dma((2, HALVES)),
            dma((2, Y)),
            dma((2, X)),
            dma((2,)),
            dma((HALVES, 2, 6)),
            dma((2, 10)),
            dma((2, R + 1)),
            dma((2, R, 2)),
            dma((2, R, 2)),
            dma((2, 2, Z)),
            dma((2, 2, Z)),
            dma((2, 2, X)),
            dma((2,)),
            dma((2,)),
        ],
        compiler_params=pltpu.CompilerParams(
            collective_id=0, has_side_effects=True, vmem_limit_bytes=58 * 1024 * 1024
        ),
        name="graph_layer",
    )(
        features,
        history,
        jnp.transpose(weights, (1, 0, 2)),
        cotangent,
        jnp.transpose(send_rows[0], (1, 0)),
        jnp.transpose(neighbors, (0, 2, 1)),
    )
    out, gf, gw = pl.pallas_call(
        hand_out,
        out_shape=tuple(jax.ShapeDtypeStruct(one.shape, one.dtype) for one in results),
        in_specs=[vmem] * 3,
        out_specs=(vmem,) * 3,
        name="hand_out",
    )(*results)
    return out, gf, jnp.transpose(gw, (1, 0, 2))


def solution(mesh):
    in_specs = (
        P("dom", None),
        P("dom", None),
        P(None, None, "mp"),
        P("dom", "mp"),
        P("dom", None, None),
        P(None, "dom", None),
    )
    out_specs = (P("dom", "mp"), P("dom", "mp"), P("dom", None, "mp"))
    chips = mesh.shape["dom"] // CORES
    X = 4 if chips >= 8 else 2
    return jax.shard_map(
        functools.partial(shards, X, chips // X), mesh=mesh, in_specs=in_specs, out_specs=out_specs, check_vma=False
    )
```

```python
import functools

import jax
import jax.numpy as jnp
from jax import lax
from jax.experimental import pallas as pl
from jax.experimental.pallas import tpu as pltpu
from jax.sharding import PartitionSpec as P

MESH = pl.DeviceIdType.MESH
CORES = 2
HALVES = 2
F32 = jnp.float32
BF16 = jnp.bfloat16


def dot(a, b):
    return jnp.dot(a, b, preferred_element_type=F32)


def dot_nt(a, b):
    return lax.dot_general(a, b, (((1,), (1,)), ((), ())), preferred_element_type=F32)


def loop(count, body):
    lax.fori_loop(0, count, lambda i, c: (body(i), c)[1], 0)


def kernel(
    X, Z, Y,
    feat_in, hist_in, w_in, cot_in, send_in, nbr_in,
    out, gf, gw,
    feat, w, cot, nbr, sendT, tcol, sendcol, histv, src, asib, aown, arecv, slabs, halo, wd, nbrcol, cnt, tab, tacc, pre, tabT,
    dp, dT, eT, bacc, gsend, gown, grecv, gx, relay, rx, gz, gzs, rz, lz, lzr, lsum, lx, lxr, bT, grad, owners, hg, ret, rets,
    in_sem, sib_sem, halo_sem, w_sem, wx_sem, wf_sem, ag1_sem, ag2_sem, gc_sem, gr_sem, gx_sem, gz_sem, lz_sem, lx_sem, ret_sem, rsib_sem,
):
    N, D = feat.shape
    R = nbr.shape[0]
    K = nbr.shape[1]
    O = w.shape[2]
    S = D // Y
    CH = X * Z
    HR = halo.shape[1]
    SL = HR // CH
    T = N + HR
    GR = gw.shape[1]
    SEND = SL // CORES

    dom = lax.axis_index("dom")
    y = lax.axis_index("mp")
    c = lax.rem(dom, CORES)
    q = dom // CORES
    z = lax.rem(q, Z)
    x = q // Z

    def at(chip, core, yy):
        return {"dom": chip * CORES + core, "mp": yy}

    def ring(v, size):
        return lax.rem(v + size, size)

    def remote(s, d, ss, rs, dev):
        return pltpu.make_async_remote_copy(
            src_ref=s, dst_ref=d, send_sem=ss, recv_sem=rs, device_id=dev, device_id_type=MESH
        )

    sibling = at(q, 1 - c, y)
    up, down, far = ring(y + 1, Y), ring(y - 1, Y), ring(y + 2, Y)

    pending = {}

    def wait(name):
        pending.pop(name)()

    def started(name, copy):
        copy.start()
        pending[name] = copy.wait_recv
        pending[name + " out"] = copy.wait_send
        return copy

    def finish():
        for one in list(pending):
            wait(one)

    columns = pl.ds(pl.multiple_of(y * S, 128), S)
    inputs = [
        ("send", send_in, sendT),
        ("feat slice", feat_in.at[:, columns], src.at[pl.ds(0, N), :]),
        ("hist", hist_in.at[:, columns], histv),
        ("w", w_in, w),
        ("nbr", nbr_in, nbr),
        ("feat", feat_in, feat),
        ("cot", cot_in, cot),
    ]

    def fetch(first, last):
        for i in range(first, last):
            name, here, there = inputs[i]
            cp = pltpu.make_async_copy(here, there, in_sem.at[i])
            cp.start()
            pending[name] = cp.wait

    fetch(0, 3)

    barrier = pltpu.get_barrier_semaphore()

    def greet(dev):
        pl.semaphore_signal(barrier, inc=1, device_id=dev, device_id_type=MESH)

    def other_chips(body):
        for dz in sorted(range(Z), key=lambda d: -min(d, Z - d)):

            def along(i):
                chip = ring(x + X // 2 + i, X) * Z + ring(z + dz, Z)
                body(chip, pl.ds(pl.multiple_of(chip * SL, SL), SL))

            if dz:
                loop(X, along)
            else:
                for i in range(X):
                    if i != X // 2:
                        along(i)

    other_chips(lambda chip, rows: greet(at(chip, c, y)))
    greet(sibling)
    for k in range(1, Y):
        greet(at(q, c, ring(y + k, Y)))

    wait("send")
    tcol[...] = jnp.transpose(sendT[...].astype(F32), (1, 0))
    even, odd = tcol[pl.ds(0, CH, stride=2), :], tcol[pl.ds(1, CH, stride=2), :]
    slot = lax.broadcasted_iota(jnp.int32, (CH, SL, SEND), 1)
    lane = lax.broadcasted_iota(jnp.int32, (CH, SL, SEND), 2)
    taken = slot == lane + c * SEND
    for k, rows in enumerate((jnp.where(c == 0, even, odd), jnp.where(c == 0, odd, even))):
        wide = jnp.broadcast_to(rows[:, None, :], (CH, SL, SEND))
        found = jnp.sum(jnp.where(taken, wide + 1.0, 0.0), axis=2, keepdims=True) - 1.0
        sendcol[k] = found.reshape(HR, 1).astype(jnp.int32)
    wait("feat slice")
    wait("hist")
    fetch(3, len(inputs))
    src[N : 2 * N, :] = histv[...].astype(BF16)

    def pick(k, dst):
        step = min(256, HR)

        def body(i):
            rows = pl.ds(i * step, step)
            col = jnp.broadcast_to(sendcol[k, rows, :].astype(jnp.int16), (step, 2 * N))
            named = col == lax.broadcasted_iota(jnp.int16, (step, 2 * N), 1)
            sel = jnp.where(named, jnp.asarray(1.0, BF16), jnp.asarray(0.0, BF16))
            dst[rows, :] = dot(sel, src[...]).astype(BF16)

        for i in range(HR // step):
            body(i)

    pick(1, asib)
    pl.semaphore_wait(barrier, CH + Y - 1)

    half = S // CORES
    piece = half // X
    half_rows = pl.ds(pl.multiple_of(c * half, half), half)
    piece_rows = pl.ds(pl.multiple_of(c * half + x * piece, piece), piece)

    def send_weights(k):
        to = ring(y + k, Y)
        rows = pl.ds(pl.multiple_of(to * S + c * half + x * piece, piece), piece)
        sems = w_sem.at[0, k], w_sem.at[1, k]
        started(f"w{k}", remote(w.at[:, rows, :], wd.at[k - 1, :, piece_rows, :], *sems, at(q, c, to)))

    def share_weights():
        for k in range(1, Y):
            wait(f"w{k}")
        part = wd.at[:, :, piece_rows, :]
        for k in range(1, X):
            to = at(ring(x + k, X) * Z + z, c, y)
            started(f"wx{k}", remote(part, part, wx_sem.at[0, k], wx_sem.at[1, k], to))

    def pass_weights():
        for k in range(1, X):
            wait(f"wx{k}")
        part = wd.at[:, :, half_rows, :]
        started("wf", remote(part, part, wf_sem.at[0], wf_sem.at[1], sibling))

    started("sib", remote(asib, arecv, sib_sem.at[0], sib_sem.at[1], sibling))
    pick(0, aown)
    wait("sib")
    slabs[...] = aown[...] + arecv[...]
    mine = pl.ds(pl.multiple_of(q * SL, SL), SL)
    halo[y, mine, :] = slabs[mine, :]

    others = pl.ds(0, HR - SL)
    part_cols = [pl.ds(h * (S // HALVES), S // HALVES) for h in range(HALVES)]
    for h, cols in enumerate(part_cols):
        sems = halo_sem.at[0, h], halo_sem.at[1, h]

        def send_slab(chip, rows):
            remote(slabs.at[rows, cols], halo.at[y, mine, cols], *sems, at(chip, c, y)).start()

        other_chips(send_slab)
        everything = remote(slabs.at[others, cols], halo.at[y, others, cols], *sems, sibling)
        pending[f"slabs{h}"] = everything.wait_recv
        pending[f"slabs{h} out"] = everything.wait_send

    wait("w")
    for k in (2, 1, 3):
        send_weights(k)

    wait("nbr")

    def counts(r):
        nbrcol[r] = jnp.transpose(nbr[r], (1, 0))
        step = min(128, N)
        share, none = jnp.asarray(1.0 / K, BF16), jnp.asarray(0.0, BF16)

        def body(i):
            rows = pl.ds(pl.multiple_of(i * step, step), step)
            cols = nbrcol[r, rows, :].astype(jnp.int16)
            pos = lax.broadcasted_iota(jnp.int16, (step, T), 1)
            total = jnp.zeros((step, T), BF16)
            for k in range(K):
                total = total + jnp.where(jnp.broadcast_to(cols[:, k : k + 1], (step, T)) == pos, share, none)
            cnt[r, rows, :] = total

        loop(N // step, body)

    def gather_start(name, buf, cols, sem):
        m = buf.shape[1] // 2
        lo, hi = pl.ds(0, m), pl.ds(m, m)
        dev_up, dev_down = at(q, c, up), at(q, c, down)

        def cp(slot, rows, k, dev):
            part = buf.at[slot, rows, cols]
            return remote(part, part, sem.at[0, k], sem.at[1, k], dev)

        copies = [
            cp(y, lo, 0, dev_up), cp(y, hi, 1, dev_down), cp(y, hi, 2, dev_up), cp(y, lo, 3, dev_down),
            cp(down, lo, 4, dev_up), cp(up, hi, 5, dev_down),
        ]
        for k in range(4):
            started(f"{name}{k}", copies[k])
        return copies

    def gather_forward(name, copies):
        wait(f"{name}0")
        started(f"{name}4", copies[4])
        wait(f"{name}1")
        started(f"{name}5", copies[5])

    def wait_halo(k):
        for h in range(HALVES):
            wait(f"halo{h}{k}")

    def local_tab(r):
        tab[r, 0:N, :] = dot(feat[...], w[r]).astype(BF16)

    def slot_rows(slot):
        return pl.ds(pl.multiple_of(slot * S, S), S)

    def turn_halo(slot):
        tabT[slot_rows(slot), N:T] = jnp.transpose(halo[slot], (1, 0))

    gathers = {}

    def gather_halo(h):
        wait(f"slabs{h}")
        gathers[h] = gather_start(f"halo{h}", halo, part_cols[h], ag1_sem.at[h])

    loop(R, counts)
    wait("feat")
    gather_halo(0)
    loop(R, local_tab)
    share_weights()
    gather_halo(1)
    gather_forward("halo0", gathers[0])

    local = dot(feat[...], w[R])
    for r in range(R):
        local = local + dot(cnt[r, :, 0:N], tab[r, 0:N, :])
    pre[...] = local
    gather_forward("halo1", gathers[1])

    def own_tab(r):
        tacc[r] = dot(halo[y], w[r, slot_rows(y), :])

    def near_tab(r):
        tacc[r] += dot(halo[down], w[r, slot_rows(down), :]) + dot(halo[up], w[r, slot_rows(up), :])

    loop(R, own_tab)
    tabT[:, 0:N] = jnp.transpose(feat[...], (1, 0))
    turn_halo(y)
    wait_halo(2)
    wait_halo(3)
    loop(R, near_tab)
    turn_halo(down)
    turn_halo(up)
    wait_halo(4)
    wait_halo(5)

    def far_tab(r):
        tab[r, N:T, :] = (tacc[r] + dot(halo[far], w[r, slot_rows(far), :])).astype(BF16)

    for r in range(R):
        far_tab(r)
    total = pre[...]
    for r in range(R):
        total = total + dot(cnt[r, :, N:T], tab[r, N:T, :])
    pre[...] = total

    wait("cot")
    tile = min(128, N)

    def activate(i):
        rows = pl.ds(pl.multiple_of(i * tile, tile), tile)
        v = pre[rows, :]
        s = 1.0 / (1.0 + jnp.exp(-v))
        out[rows, :] = (v * s).astype(BF16)
        dp[y, rows, :] = (cot[rows, :].astype(F32) * (s * (1.0 + v * (1.0 - s)))).astype(BF16)

    loop(N // tile, activate)
    ag2 = [
        remote(dp.at[slot, rows, :], dp.at[slot, rows, :], ag2_sem.at[0, k], ag2_sem.at[1, k], at(q, c, to))
        for k, (slot, first, count, to) in enumerate((
            (y, 0, 1, up), (y, 2, 1, down), (y, 1, 1, up), (y, 3, 1, down), (y, 2, 2, up), (y, 0, 2, down),
            (down, 0, 1, up), (up, 2, 1, down), (down, 1, 1, up), (up, 3, 1, down),
        ))
        for rows in [pl.ds(first * (N // 4), count * (N // 4))]
    ]
    for k in range(6):
        started(f"dp{k}", ag2[k])

    def forward_dp(k):
        wait(f"dp{k}")
        started(f"dp{k + 6}", ag2[k + 6])

    dT[...] = jnp.transpose(dp[y], (1, 0))
    turn_halo(far)

    def core_copy(p):
        return remote(gsend.at[p], grecv.at[p], gc_sem.at[0, p], gc_sem.at[1, p], sibling)

    def put_terms(p, part):
        part = part.reshape(CH, CORES, GR, O)
        gown[p] = jnp.where(c == 0, part[:, 0], part[:, 1])
        gsend[p] = jnp.where(c == 0, part[:, 1], part[:, 0]).astype(BF16)
        started(f"core{p}", core_copy(p))

    def relation_terms(r):
        eT[r] = dot(dT[...], cnt[r]).astype(BF16)
        put_terms(r + 1, dot_nt(tabT[...], eT[r]))

    x_up, x_down, x_far = ring(x + 1, X), ring(x - 1, X), ring(x + 2, X)
    zh = Z // 2

    def x_copy(p, k, block, to):
        return remote(block, rx.at[p, k], gx_sem.at[0, p, k], gx_sem.at[1, p, k], at(to * Z + z, c, y))

    def far_x(p):
        wait(f"core{p}")
        some = min(8, CH)

        def body(i):
            chips = pl.ds(i * some, some)
            total = gown[p, chips] + grecv[p, chips].astype(F32)
            gown[p, chips] = total
            gx[p, chips] = total.astype(BF16)

        loop(CH // some, body)
        for k, to in enumerate((x_up, x_down)):
            block = gx.at[p, pl.ds(x_far * Z + k * zh, zh)]
            sems = gr_sem.at[0, p, k], gr_sem.at[1, p, k]
            started(f"r{p}{k}", remote(block, relay.at[p, k], *sems, at(to * Z + z, c, y)))

    def near_x(p):
        for k, to in enumerate((x_up, x_down)):
            wait(f"r{p}{k}")
            part = pl.ds(to * Z + k * zh, zh)
            gx[p, part] = (gown[p, part] + relay[p, k].astype(F32)).astype(BF16)
            started(f"x{p}{k}", x_copy(p, k, gx.at[p, pl.ds(to * Z, Z)], to))

    z_first = (0, R)

    def far_z(l):
        p = z_first[l]
        wait(f"core{p}")

        def body(i):
            chips = pl.ds(i * Z, Z)
            total = gown[p, chips] + grecv[p, chips].astype(F32)
            gown[p, chips] = total
            lz[l, i] = total.astype(BF16)

        loop(X, body)
        for k in range(1, Z):
            to = ring(z + k, Z)
            sems = lz_sem.at[l, 0, k], lz_sem.at[l, 1, k]
            started(f"lz{l}{k}", remote(lz.at[l, :, to], lzr.at[l, k - 1], *sems, at(x * Z + to, c, y)))

    def near_z(l):
        for k in range(1, Z):
            wait(f"lz{l}{k}")

        def body(i):
            total = gown[z_first[l], i * Z + z]
            for k in range(1, Z):
                total = total + lzr[l, k - 1, i].astype(F32)
            lsum[l, i] = total
            lx[l, i] = total.astype(BF16)

        loop(X, body)
        for k in range(1, X):
            to = ring(x + k, X)
            sems = lx_sem.at[l, 0, k], lx_sem.at[l, 1, k]
            started(f"lx{l}{k}", remote(lx.at[l, to], lxr.at[l, k - 1], *sems, at(to * Z + z, c, y)))

    put_terms(0, dot(tabT[:, 0:N], dp[y]))
    relation_terms(0)
    far_z(0)
    for r in range(1, R):
        relation_terms(r)
        far_x(r)
        if r == R - 2:
            forward_dp(0)
            forward_dp(1)
    forward_dp(2)
    forward_dp(3)
    far_z(1)
    pass_weights()

    def own_back(r):
        bacc[r] = dot_nt(w[r, slot_rows(y), :], dp[y])

    def near_back(r):
        bacc[r] += dot_nt(wd[0, r], dp[down]) + dot_nt(wd[2, r], dp[up])

    def far_back(r):
        bT[r] = (bacc[r] + dot_nt(wd[1, r], dp[far])).astype(BF16)

    loop(R + 1, own_back)
    for p in range(1, R):
        near_x(p)
    wait("wf")
    for k in (4, 5):
        wait(f"dp{k}")
    loop(R + 1, near_back)
    for k in (6, 7, 8, 9):
        wait(f"dp{k}")
    for r in range(R):
        far_back(r)
    received = dot(bT[0], cnt[0, :, N:T])
    for r in range(1, R):
        received = received + dot(bT[r], cnt[r, :, N:T])

    hg[...] = jnp.transpose(received, (1, 0)).astype(BF16)
    ret[mine, :] = hg[mine, :]

    def return_slab(chip, rows):
        remote(hg.at[rows, :], ret.at[mine, :], ret_sem.at[0], ret_sem.at[1], at(chip, c, y)).start()

    other_chips(return_slab)
    ret_all = remote(hg.at[others, :], ret.at[others, :], ret_sem.at[0], ret_sem.at[1], sibling)
    pending["ret"] = ret_all.wait_recv
    pending["ret out"] = ret_all.wait_send

    def z_copy(g, places, k):
        to = ring(z + k, Z)
        return remote(
            gzs.at[places, to], rz.at[k - 1, places], gz_sem.at[0, g, k], gz_sem.at[1, g, k], at(x * Z + to, c, y)
        )

    def along_z(g, first, last):
        for p in range(first, last):
            total = gown[p, pl.ds(x * Z, Z)]
            for k in range(2):
                wait(f"x{p}{k}")
                total = total + rx[p, k].astype(F32)
            gz[p] = total
            gzs[p] = total.astype(BF16)
        for k in range(1, Z):
            started(f"z{g}{k}", z_copy(g, pl.ds(first, last - first), k))

    near_z(0)
    along_z(0, 1, R - 1)

    own = bacc[R] + dot_nt(wd[1, R], dp[far])
    for r in range(R):
        own = own + dot(bT[r], cnt[r, :, 0:N])
    grad[...] = jnp.transpose(own, (1, 0))

    def owner_map(k):
        rows = lax.broadcasted_iota(jnp.int32, (N, HR), 0)
        named = jnp.transpose(jnp.broadcast_to(sendcol[k], (HR, 8)), (1, 0))[0:1]
        return jnp.where(named == rows, 1.0, 0.0).astype(BF16)

    near_z(1)
    along_z(1, R - 1, R)
    for k in range(2):
        owners[k] = owner_map(k)

    for name in [name for name in pending if name.endswith(" out") and not name.startswith(("ret", "z", "l"))]:
        wait(name)
    wait("ret")
    started("rets", remote(ret, rets, rsib_sem.at[0], rsib_sem.at[1], sibling))
    grad[...] += dot(owners[0], ret[...])
    wait("rets")
    gf[...] = (grad[...] + dot(owners[1], rets[...])).astype(BF16)

    def total_terms(p, r):
        total = gz[p, z]
        for k in range(1, Z):
            total = total + rz[k - 1, p].astype(F32)
        gw[r] = total

    for k in range(1, Z):
        wait(f"z0{k}")
        wait(f"z1{k}")
    loop(R - 1, lambda r: total_terms(r + 1, r))
    for l, r in enumerate((R, R - 1)):
        last = lsum[l, x]
        for k in range(1, X):
            wait(f"lx{l}{k}")
            last = last + lxr[l, k - 1].astype(F32)
        gw[r] = last
    finish()


def hand_out(*refs):
    for here, there in zip(refs[:3], refs[3:]):
        there[...] = here[...]


def shards(X, Z, features, history, weights, cotangent, send_rows, neighbors):
    N, D = features.shape
    R, _, K = neighbors.shape
    O = weights.shape[2]
    Y = lax.axis_size("mp")
    S = D // Y
    CH = X * Z
    SL = CORES * send_rows.shape[2]
    HR = CH * SL
    T = N + HR
    GR = D // (CH * CORES)

    dma = pltpu.SemaphoreType.DMA
    vmem = pl.BlockSpec(memory_space=pltpu.VMEM)
    anywhere = pl.BlockSpec(memory_space=pl.ANY)
    results = pl.pallas_call(
        functools.partial(kernel, X, Z, Y),
        out_shape=(
            jax.ShapeDtypeStruct((N, O), BF16),
            jax.ShapeDtypeStruct((N, S), BF16),
            jax.ShapeDtypeStruct((R + 1, GR, O), F32),
        ),
        in_specs=[anywhere] * 6,
        out_specs=(vmem, vmem, vmem),
        scratch_shapes=[
            pltpu.VMEM((N, D), BF16),
            pltpu.VMEM((R + 1, D, O), BF16),
            pltpu.VMEM((N, O), BF16),
            pltpu.VMEM((R, K, N), jnp.int32),
            pltpu.VMEM((SL // CORES, CH * CORES), jnp.int32),
            pltpu.VMEM((CH * CORES, SL // CORES), F32),
            pltpu.VMEM((2, HR, 1), jnp.int32),
            pltpu.VMEM((N, S), F32),
            pltpu.VMEM((2 * N, S), BF16),
            pltpu.VMEM((HR, S), BF16),
            pltpu.VMEM((HR, S), BF16),
            pltpu.VMEM((HR, S), BF16),
            pltpu.VMEM((HR, S), BF16),
            pltpu.VMEM((Y, HR, S), BF16),
            pltpu.VMEM((Y - 1, R + 1, S, O), BF16),
            pltpu.VMEM((R, N, K), jnp.int32),
            pltpu.VMEM((R, N, T), BF16),
            pltpu.VMEM((R, T, O), BF16),
            pltpu.VMEM((R, HR, O), F32),
            pltpu.VMEM((N, O), F32),
            pltpu.VMEM((D, T), BF16),
            pltpu.VMEM((Y, N, O), BF16),
            pltpu.VMEM((O, N), BF16),
            pltpu.VMEM((R, O, T), BF16),
            pltpu.VMEM((R + 1, S, N), F32),
            pltpu.VMEM((R + 1, CH, GR, O), BF16),
            pltpu.VMEM((R + 1, CH, GR, O), F32),
            pltpu.VMEM((R + 1, CH, GR, O), BF16),
            pltpu.VMEM((R, CH, GR, O), BF16),
            pltpu.VMEM((R, 2, Z // 2, GR, O), BF16),
            pltpu.VMEM((R, 2, Z, GR, O), BF16),
            pltpu.VMEM((R, Z, GR, O), F32),
            pltpu.VMEM((R, Z, GR, O), BF16),
            pltpu.VMEM((Z - 1, R, GR, O), BF16),
            pltpu.VMEM((2, X, Z, GR, O), BF16),
            pltpu.VMEM((2, Z - 1, X, GR, O), BF16),
            pltpu.VMEM((2, X, GR, O), F32),
            pltpu.VMEM((2, X, GR, O), BF16),
            pltpu.VMEM((2, X - 1, GR, O), BF16),
            pltpu.VMEM((R, S, N), BF16),
            pltpu.VMEM((N, S), F32),
            pltpu.VMEM((2, N, HR), BF16),
            pltpu.VMEM((HR, S), BF16),
            pltpu.VMEM((HR, S), BF16),
            pltpu.VMEM((HR, S), BF16),
            dma((7,)),
            dma((2,)),
            dma((2, HALVES)),
            dma((2, Y)),
            dma((2, X)),
            dma((2,)),
            dma((HALVES, 2, 6)),
            dma((2, 10)),
            dma((2, R + 1)),
            dma((2, R, 2)),
            dma((2, R, 2)),
            dma((2, 2, Z)),
            dma((2, 2, Z)),
            dma((2, 2, X)),
            dma((2,)),
            dma((2,)),
        ],
        compiler_params=pltpu.CompilerParams(
            collective_id=0, has_side_effects=True, vmem_limit_bytes=58 * 1024 * 1024
        ),
        name="graph_layer",
    )(
        features,
        history,
        jnp.transpose(weights, (1, 0, 2)),
        cotangent,
        jnp.transpose(send_rows[0], (1, 0)),
        jnp.transpose(neighbors, (0, 2, 1)),
    )
    out, gf, gw = pl.pallas_call(
        hand_out,
        out_shape=tuple(jax.ShapeDtypeStruct(one.shape, one.dtype) for one in results),
        in_specs=[vmem] * 3,
        out_specs=(vmem,) * 3,
        name="hand_out",
    )(*results)
    return out, gf, jnp.transpose(gw, (1, 0, 2))


def solution(mesh):
    in_specs = (
        P("dom", None),
        P("dom", None),
        P(None, None, "mp"),
        P("dom", "mp"),
        P("dom", None, None),
        P(None, "dom", None),
    )
    out_specs = (P("dom", "mp"), P("dom", "mp"), P("dom", None, "mp"))
    chips = mesh.shape["dom"] // CORES
    X = 4 if chips >= 8 else 2
    return jax.shard_map(
        functools.partial(shards, X, chips // X), mesh=mesh, in_specs=in_specs, out_specs=out_specs, check_vma=False
    )
```
